32 devices in a mesh: group: 2 (over y), stn: 4 (over z), tm: 2 (over x), pol: 2 (over core).
Axes of the slice: x: 2, y: 2, z: 4, core: 2. Of those that a mesh axis runs over, the one named last changes fastest.
Arguments:
- voltages: bfloat16 [512, 2, 55, 4096], P(('group', 'stn', 'tm'), 'pol'), parts along dimension 0, may hold values from -6 to 6
- fir_taps: bfloat16 [8, 2048], replicated, may hold values from -1.5 to 1.5
- owner_map: int32 [32, 1], replicated, may hold values from 0 to 7; in each aligned block of 32 rows (0 to 31, 32 to 63, ...) at most 8 rows name the same one
- station_flag_marks: int32 [256], P(('stn', 'tm')), may hold values 0 or 1
Outputs:
- visibilities: bfloat16 [16, 8, 2, 512, 512], P(('group', 'stn', 'tm'), None, None, 'pol'), parts along dimension 0
The draws below stay inside these ranges and needn't reach their ends.
There are 2 independent parts, one for each index of `group`. The reference program is written for one: setup_inputs(seed, part) draws one part's arguments, and reference() takes and returns one part's arrays. A program takes and returns all parts, laid end to end along the dimension named above; an argument that names none is the same for every part. Nothing has to cross between parts.
Inputs may be any that keep to these rules, and one draw needn't show every extreme that they name: `owner_map`: no owner has more than 8 channels, some owner has exactly 8, and every owner has at least one.
All inputs are finite; a program needn't handle non-finite values. No bound on the sum of `station_flag_marks` on one device may be relied on, other than what follows from the above.
Results may differ from the reference program's by a relative error of at most 0.008.
Values may be sent and summed in bfloat16 or wider, within the bound.
A program may use at most 64 MiB of HBM per device.

```python
import math
import jax
import jax.numpy as jnp
import numpy as np
from jax import lax

STATIONS = 256
NFFT = 2048
TAPS = 8
NB = 48
CH = 32
SPAN = 55
CAP = 8
N_STN = 4
N_TM = 2


def touch_ends(array, key, smallest, largest):
    shape = array.shape
    place = [jax.random.randint(jax.random.fold_in(key, axis), (), 0, shape[axis]) for axis in range(len(shape))]
    array = array.at[tuple(place)].set(smallest)
    longest = shape.index(max(shape))
    place[longest] = (place[longest] + 1) % shape[longest]
    return array.at[tuple(place)].set(largest)


def steps_of(stream_key, shape, split, low, largest):
    def one(dim, blocks):
        heights = jax.random.uniform(jax.random.fold_in(jax.random.fold_in(stream_key, 6), dim), (blocks,), jnp.float32, low / len(split), largest / len(split))
        return jnp.repeat(jnp.exp(heights), shape[dim] // blocks).reshape((-1,) + (1,) * (len(shape) - dim - 1))

    factor_of = one(*split[0])
    for cut in split[1:]:
        factor_of = factor_of * one(*cut)
    return factor_of


def routed_block(stream_key, own, number, rows, amount, top, reach, slope):
    order = jax.random.permutation(stream_key, amount)
    heavy_load, usual = portions_of(amount, rows * top, reach, slope, True), portions_of(amount, rows * top, reach, slope, False)
    places = jnp.arange(amount)

    def named(tallies, offset_by):
        used = int((tallies > 0).sum())
        fixed = max(1, used // 4)
        moved = fixed + (places - fixed + offset_by * (used - fixed)) % max(1, amount - fixed)
        return jnp.zeros((amount,), jnp.int32).at[order[jnp.where(places < fixed, places, moved)]].set(jnp.asarray(tallies, jnp.int32))

    tallies = jnp.where(number % 4 == 0, named(heavy_load, number // 4), named(usual, number - number // 4 - 1))
    mixed = jax.random.permutation(jax.random.fold_in(own, 3), amount)
    source_of, taker = mixed[0:amount // 2 * 2:2], mixed[1:amount // 2 * 2:2]
    room = jnp.minimum(tallies[source_of] - 1, reach - tallies[taker]) // 2
    room = jnp.where((source_of == order[0]) | (taker == order[0]) | (tallies[taker] == 0), 0, jnp.maximum(room, 0))
    moved = jax.random.randint(jax.random.fold_in(own, 4), (amount // 2,), 0, 1 << 20) % (room + 1)
    tallies = tallies.at[source_of].add(-moved).at[taker].add(moved)
    items = jnp.searchsorted(jnp.cumsum(tallies), jnp.arange(rows * top), side="right").astype(jnp.int32)
    table = items.reshape(top, rows).T
    table = table[jax.random.permutation(jax.random.fold_in(own, 1), rows)]
    offset_by = jax.random.randint(jax.random.fold_in(own, 2), (rows, 1), 0, top)
    return jnp.take_along_axis(table, (jnp.arange(top)[None, :] + offset_by) % top, axis=1)


def portions_of(number_of, total, reach, lean, full):
    portions = [(1 << 20) // math.isqrt(rank ** lean) + 1 for rank in range(1, number_of + 1)]
    largest = reach if full else min(reach, max(-(-total // number_of), total * portions[0] // sum(portions)))
    least = 1 if total - largest >= number_of - 1 else 0
    given, rest = [largest] + [least] * (number_of - 1), total - largest - least * (number_of - 1)
    while rest > 0:
        candidates = [i for i in range(1, number_of) if given[i] < largest] or [i for i in range(1, number_of) if given[i] < reach]
        mass, remaining = sum([portions[i] for i in candidates]), rest
        for i in candidates:
            addition = min(reach - given[i], max(1, remaining * portions[i] // mass), rest)
            given[i] = given[i] + addition
            rest = rest - addition
    return np.array(given)


def bell_draw(stream_key, extent, deviation, bound, cuts=(), held_as=jnp.bfloat16):
    entries = jax.random.normal(stream_key, extent, jnp.float32) * deviation
    if len(cuts) > 0:
        entries = steps_of(stream_key, extent, cuts, -0.22, 0.18) * entries
    return jnp.clip(entries, min=-bound, max=bound).astype(held_as)


def setup_inputs(seed: int = 0, part: int = 0) -> dict:
    key_list = jax.random.split(jax.random.key(seed), 5)
    part_keys = jax.random.split(jax.random.fold_in(key_list[4], part), 5)
    voltages = bell_draw(part_keys[0], (STATIONS, 2, SPAN, 2 * NFFT), 1.0, 6.0, ((0, 8), (1, 2)))
    fir_taps = bell_draw(key_list[1], (TAPS, NFFT), 0.25, 1.5)
    owner_map_keys = jax.random.split(jax.random.fold_in(key_list[2], 1), CH // CH)
    owner_map_turns = jax.random.permutation(jax.random.fold_in(key_list[2], 3), CH // CH)
    owner_map = jax.vmap(lambda own, number: routed_block(jax.random.fold_in(key_list[2], 2), own, number, CH, N_STN * N_TM, 1, CAP, 2))(owner_map_keys, owner_map_turns).reshape((CH, 1))
    station_flag_marks = touch_ends((jax.random.randint(key_list[3], (STATIONS,), 0, 8) < 1).astype(jnp.int32), jax.random.fold_in(key_list[3], 1), 0, 1)
    return {"voltages": voltages, "fir_taps": fir_taps, "owner_map": owner_map, "station_flag_marks": station_flag_marks}


def dft_table(fft_length, channels):
    row_numbers = jnp.arange(fft_length, dtype=jnp.int32)[:, None]
    col_ids = jnp.arange(channels, dtype=jnp.int32)[None, :]
    phase_idx = (row_numbers * col_ids % fft_length).astype(jnp.float32) * (2.0 * math.pi / fft_length)
    norm_scale = 1.0 / math.sqrt(fft_length)
    cosine = (jnp.cos(phase_idx) * norm_scale).astype(jnp.bfloat16)
    sine_part = (jnp.sin(phase_idx) * norm_scale).astype(jnp.bfloat16)
    upper_rows = jnp.concatenate([cosine, -sine_part], axis=1)
    lower_rows = jnp.concatenate([sine_part, cosine], axis=1)
    return jnp.concatenate([upper_rows, lower_rows], axis=0)

def slot_matches(route_map, owners, capacity):
    channels = route_map.shape[0]
    position = jnp.arange(channels, dtype=jnp.int32)
    earlier = (route_map[:, None] == route_map[None, :]) & (position[None, :] < position[:, None])
    position_within_owner = lax.optimization_barrier(jnp.sum(earlier.astype(jnp.int32), axis=1))
    owner_ids = jnp.arange(owners, dtype=jnp.int32)
    slot_ids = jnp.arange(capacity, dtype=jnp.int32)
    return (route_map[None, None, :] == owner_ids[:, None, None]) & (position_within_owner[None, None, :] == slot_ids[None, :, None])

def reference(voltages, fir_taps, owner_map, station_flag_marks):
    table = dft_table(NFFT, CH)
    wide_taps = jnp.concatenate([fir_taps, fir_taps], axis=1).astype(jnp.float32)
    clean_stations = (1 - station_flag_marks).astype(jnp.float32)

    def split_into_channels(operands):
        samples, keep_one = operands
        filtered = wide_taps[0] * samples[:, 0:NB].astype(jnp.float32)
        for tap_index in range(1, TAPS):
            filtered = filtered + wide_taps[tap_index] * samples[:, tap_index:tap_index + NB].astype(jnp.float32)
        flat_rows = filtered.astype(jnp.bfloat16).reshape(2 * NB, 2 * NFFT)
        single_spectrum = jnp.dot(flat_rows, table, preferred_element_type=jnp.float32) * keep_one
        return single_spectrum.astype(jnp.bfloat16).reshape(2, NB, 2, CH)
    channel_spectra = lax.map(split_into_channels, (voltages, clean_stations))
    signal = jnp.transpose(channel_spectra, (4, 3, 1, 0, 2)).reshape(CH, 2, 2 * STATIONS, NB)

    def correlate(signal_one):
        real_rows = signal_one[0]
        imag_rows = signal_one[1]
        real_real = jnp.dot(real_rows, real_rows.T, preferred_element_type=jnp.float32)
        imag_imag = jnp.dot(imag_rows, imag_rows.T, preferred_element_type=jnp.float32)
        imag_real = jnp.dot(imag_rows, real_rows.T, preferred_element_type=jnp.float32)
        real_imag = jnp.dot(real_rows, imag_rows.T, preferred_element_type=jnp.float32)
        real_part = (real_real + imag_imag) / NB
        imag_part = (imag_real - real_imag) / NB
        return jnp.stack([real_part, imag_part]).astype(jnp.bfloat16)
    gram_all = lax.map(correlate, signal)
    owners = N_STN * N_TM
    matches = slot_matches(owner_map[:, 0], owners, CAP)
    position = jnp.arange(CH, dtype=jnp.int32)
    slot_channel = lax.optimization_barrier(jnp.sum(jnp.where(matches, position[None, None, :], 0), axis=2)).astype(jnp.int32)
    slot_used = jnp.any(matches, axis=2)
    picked = jnp.take(gram_all, slot_channel.reshape(-1), axis=0).reshape(owners, CAP, 2, 2 * STATIONS, 2 * STATIONS)
    return jnp.where(slot_used[:, :, None, None, None], picked, jnp.zeros_like(picked))
```

```python
import functools
import math

import jax
import jax.numpy as jnp
import numpy as np
from jax import lax
from jax.experimental import pallas as pl
from jax.experimental.pallas import tpu as pltpu
from jax.sharding import PartitionSpec as P


def partner(value, axis, stride):
    return lax.ppermute(value, axis, [(i, i ^ 1 << stride) for i in range(lax.axis_size(axis))])


def dft_table(fft_length, channels):
    row_numbers = jnp.arange(fft_length, dtype=jnp.int32)[:, None]
    col_ids = jnp.arange(channels, dtype=jnp.int32)[None, :]
    phase_idx = (row_numbers * col_ids % fft_length).astype(jnp.float32) * (
        2.0 * math.pi / fft_length
    )
    norm_scale = 1.0 / math.sqrt(fft_length)
    cosine = (jnp.cos(phase_idx) * norm_scale).astype(jnp.bfloat16)
    sine_part = (jnp.sin(phase_idx) * norm_scale).astype(jnp.bfloat16)
    upper_rows = jnp.concatenate([cosine, -sine_part], axis=1)
    lower_rows = jnp.concatenate([sine_part, cosine], axis=1)
    return jnp.concatenate([upper_rows, lower_rows], axis=0)


def slot_matches(route_map, owners, capacity):
    channels = route_map.shape[0]
    position = jnp.arange(channels, dtype=jnp.int32)
    earlier = (route_map[:, None] == route_map[None, :]) & (position[None, :] < position[:, None])
    position_within_owner = jnp.sum(earlier.astype(jnp.int32), axis=1)
    owner_ids = jnp.arange(owners, dtype=jnp.int32)
    slot_ids = jnp.arange(capacity, dtype=jnp.int32)
    return (route_map[None, None, :] == owner_ids[:, None, None]) & (
        position_within_owner[None, None, :] == slot_ids[None, :, None]
    )


def corner_turn(outgoing):
    return lax.all_to_all(outgoing, ("stn", "tm"), split_axis=3, concat_axis=3, tiled=True)


def general_body(voltages, fir_taps, owner_map, station_flag_marks):
    st_dev = voltages.shape[0]
    span_blocks = voltages.shape[2]
    fft_length = voltages.shape[3] // 2
    tap_count = fir_taps.shape[0]
    blocks = span_blocks - tap_count + 1
    channels = owner_map.shape[0]
    stn_count = lax.axis_size("stn")
    tm_count = lax.axis_size("tm")
    owners = stn_count * tm_count
    capacity = 2 * channels // owners
    stations = st_dev * owners
    pol_index = lax.axis_index("pol")
    table = dft_table(fft_length, channels)
    wide_taps = jnp.concatenate([fir_taps, fir_taps], axis=1).astype(jnp.float32)
    samples = voltages[:, 0]
    filtered = wide_taps[0] * samples[:, 0:blocks].astype(jnp.float32)
    for tap_index in range(1, tap_count):
        filtered = filtered + wide_taps[tap_index] * samples[
            :, tap_index : tap_index + blocks
        ].astype(jnp.float32)
    flat_rows = filtered.astype(jnp.bfloat16).reshape(st_dev * blocks, 2 * fft_length)
    single_spectrum = jnp.dot(flat_rows, table, preferred_element_type=jnp.float32).reshape(
        st_dev, blocks, 2, channels
    )
    clean_stations = (1 - station_flag_marks).astype(jnp.float32)
    channel_spectra = (single_spectrum * clean_stations[:, None, None, None]).astype(jnp.bfloat16)
    pick_matrix = slot_matches(owner_map[:, 0], owners, capacity).astype(jnp.bfloat16)
    outgoing = jnp.einsum(
        "okc,sbqc->kqosb", pick_matrix, channel_spectra, preferred_element_type=jnp.float32
    )
    outgoing = outgoing.astype(jnp.bfloat16).reshape(capacity, 2, 1, owners, st_dev * blocks)
    arrived = corner_turn(outgoing)
    row_block = arrived.reshape(capacity, 2, stations, blocks)
    other_block = partner(row_block, "pol", 0)
    col_block = jnp.where(
        pol_index == 0,
        jnp.concatenate([row_block, other_block], axis=2),
        jnp.concatenate([other_block, row_block], axis=2),
    )
    products = jnp.einsum(
        "kqib,krjb->kqrij", row_block, col_block, preferred_element_type=jnp.float32
    )
    real_part = (products[:, 0, 0] + products[:, 1, 1]) / blocks
    imag_part = (products[:, 1, 0] - products[:, 0, 1]) / blocks
    return jnp.stack([real_part, imag_part], axis=1).astype(jnp.bfloat16)[None]


GROUP = 8
STEP = 16
LANES = 128


def wide_table(fft_length, channels):
    n = np.arange(fft_length, dtype=np.int64)[:, None]
    k = np.arange(channels, dtype=np.int64)[None, :]
    phase = (n * k % fft_length).astype(np.float32) * np.float32(2.0 * math.pi / fft_length)
    scale = np.float32(1.0 / math.sqrt(fft_length))
    cosine = (np.cos(phase) * scale).astype(jnp.bfloat16)
    sine = (np.sin(phase) * scale).astype(jnp.bfloat16)
    upper = np.concatenate([cosine, -sine], axis=1)
    lower = np.concatenate([sine, cosine], axis=1)
    whole = np.concatenate([upper, lower], axis=0)
    return np.concatenate([whole] * (LANES // (2 * channels)), axis=1)


def iota(shape, dim):
    return lax.broadcasted_iota(jnp.int32, shape, dim)


def slot_columns(owner_ref, channels, capacity):
    col = owner_ref[...]
    lane = iota((channels, LANES), 1)
    channel = lane % channels
    row_number = iota((channels, LANES), 0)
    owner = jnp.sum(jnp.where(row_number == channel, col, 0), axis=0, keepdims=True)
    rank = jnp.sum(
        jnp.where((col == owner) & (row_number < channel), 1, 0), axis=0, keepdims=True
    )
    lane = iota((1, LANES), 1)
    place = (owner * capacity + rank) * 2 + lane // channels
    place = jnp.where(lane < 2 * channels, place, -1)
    hot = jnp.where(iota((LANES, LANES), 0) == place, 1.0, 0.0)
    return hot.T.astype(jnp.bfloat16)


def block_transpose(parts, width):
    count = len(parts)
    lane = iota(parts[0].shape, 1) // width
    half = 1
    while half < count:
        low = lane // half % 2 == 0
        out = list(parts)
        for i in range(count):
            if i // half % 2 == 0:
                a, b = parts[i], parts[i + half]
                out[i] = jnp.where(low, a, pltpu.roll(b, half * width, 1))
                out[i + half] = jnp.where(low, pltpu.roll(a, LANES - half * width, 1), b)
        parts = out
        half *= 2
    return parts


def channelize_kernel(
    sizes, v_ref, taps_ref, table_ref, owner_ref, marks_ref, x_ref,
    vbuf, tail, wbuf, zbuf, sendbuf, in_sem, send_sem, recv_sem, own_sem, pass_send, pass_recv,
):
    stations, span, samples, taps, blocks, channels, owners, capacity, tm_count = sizes
    steps = -(-span // STEP)
    groups = blocks // GROUP
    width = 2 * capacity
    pol = lax.axis_index("pol")
    me = lax.axis_index("stn") * tm_count + lax.axis_index("tm")

    loads = []
    for c in range(steps):
        rows = min(STEP, span - c * STEP)
        load = pltpu.make_async_copy(
            v_ref.at[:, 0, pl.ds(c * STEP, rows), :],
            vbuf.at[c] if rows == STEP else tail,
            in_sem.at[c],
        )
        load.start()
        loads.append(load)

    barrier = pltpu.get_barrier_semaphore()
    for k in range(1, owners):
        peer = lax.rem(me + k, owners)
        pl.semaphore_signal(
            barrier, inc=1, device_id={"stn": peer // tm_count, "tm": lax.rem(peer, tm_count)},
            device_id_type=pl.DeviceIdType.MESH,
        )
    pl.semaphore_signal(
        barrier, inc=1, device_id={"pol": 1 - pol}, device_id_type=pl.DeviceIdType.MESH
    )

    columns = taps * 2 * channels
    expand = jnp.where(
        iota((taps, columns), 0) == iota((taps, columns), 1) // (2 * channels), 1.0, 0.0
    ).astype(jnp.bfloat16)
    half = samples // 2
    piece = 256
    for i in range(half // piece):
        tap_rows = lax.dot_general(
            taps_ref[:, i * piece : (i + 1) * piece], expand,
            (((0,), (0,)), ((), ())), preferred_element_type=jnp.float32,
        )
        for base in (0, half):
            at = slice(base + i * piece, base + (i + 1) * piece)
            entry = table_ref[at, :].astype(jnp.float32)
            for j in range(columns // LANES):
                lanes = slice(j * LANES, (j + 1) * LANES)
                wbuf[at, lanes] = (tap_rows[:, lanes] * entry).astype(jnp.bfloat16)

    pick = slot_columns(owner_ref, channels, capacity)
    diagonal = iota((stations, stations), 0) == iota((stations, stations), 1)
    keep = 1.0 - jnp.sum(
        jnp.where(diagonal, marks_ref[...], 0), axis=1, keepdims=True
    ).astype(jnp.float32)
    pl.semaphore_wait(barrier, owners)

    def shifted(b):
        total = None
        for j in range(columns // LANES):
            row = b + 2 * j
            first = row // STEP * stations * STEP + row % STEP
            term = zbuf[j, pl.ds(first, stations, stride=STEP), :]
            total = term if total is None else total + term
        return total

    sends, passes = [], []

    def send_groups(c, first, last):
        lanes = pl.ds(first * LANES, (last - first) * LANES)
        rows = pl.ds(me * stations, stations)
        for g in range(first, last):
            summed = [shifted(g * GROUP + i) for i in range(GROUP + 1)]
            spectra = [
                ((summed[i] + pltpu.roll(summed[i + 1], 2 * channels, 1)) * keep).astype(jnp.bfloat16)
                for i in range(GROUP)
            ]
            placed = jnp.dot(
                jnp.concatenate(spectra, axis=0), pick, preferred_element_type=jnp.float32
            )
            parts = [placed[i * stations : (i + 1) * stations] for i in range(GROUP)]
            for o, part in enumerate(block_transpose(parts, width)):
                sendbuf[o, :, g * LANES : (g + 1) * LANES] = part.astype(jnp.bfloat16)
        batch = []
        for k in range(1, owners):
            peer = lax.rem(me + k, owners)
            copy = pltpu.make_async_remote_copy(
                src_ref=sendbuf.at[peer, :, lanes],
                dst_ref=x_ref.at[pol, rows, lanes],
                send_sem=send_sem.at[c, k],
                recv_sem=recv_sem.at[c, k],
                device_id={"stn": peer // tm_count, "tm": lax.rem(peer, tm_count)},
                device_id_type=pl.DeviceIdType.MESH,
            )
            copy.start()
            batch.append(copy)
        own = pltpu.make_async_copy(
            sendbuf.at[me, :, lanes], x_ref.at[pol, rows, lanes], own_sem.at[c]
        )
        own.start()
        sends.append((batch, own, lanes))

    def pass_on(c):
        batch, own, lanes = sends[c]
        own.wait()
        for k in range(1, owners):
            source = lax.rem(me + owners - k, owners)
            here = x_ref.at[pol, pl.ds(source * stations, stations), lanes]
            pltpu.make_async_copy(here, here, recv_sem.at[c, k]).wait()
        mine = x_ref.at[pol, :, lanes]
        copy = pltpu.make_async_remote_copy(
            src_ref=mine, dst_ref=mine, send_sem=pass_send.at[c], recv_sem=pass_recv.at[c],
            device_id={"pol": 1 - pol}, device_id_type=pl.DeviceIdType.MESH,
        )
        copy.start()
        passes.append(copy)

    done = 0
    for c in range(steps):
        loads[c].wait()
        if span - c * STEP < STEP:
            vbuf[c, :, 0 : tail.shape[1], :] = tail[...]
        product = jnp.dot(
            vbuf[c].reshape(stations * STEP, samples), wbuf[...],
            preferred_element_type=jnp.float32,
        )
        for j in range(columns // LANES):
            zbuf[j, c * stations * STEP : (c + 1) * stations * STEP, :] = product[
                :, j * LANES : (j + 1) * LANES
            ]
        if c >= 1:
            pass_on(c - 1)
        ready = min(groups, (min(span, (c + 1) * STEP) - taps + 1) // GROUP)
        send_groups(c, done, ready)
        done = ready
    pass_on(steps - 1)
    for batch, own, lanes in sends:
        for copy in batch:
            copy.wait_send()
    for copy in passes:
        copy.wait()


def correlate_kernel(blocks, capacity, x_ref, out_ref, held):
    k = pl.program_id(0)
    pol = lax.axis_index("pol")
    rows, depth = x_ref.shape[1], x_ref.shape[2]
    lane = iota((1, 2 * LANES), 1)
    swapped = lane // LANES
    inner = lane % LANES
    part = inner // blocks
    wanted = inner % blocks * (2 * capacity) + 2 * k + jnp.where(swapped == 1, 1 - part, part)
    wanted = jnp.where(inner < 2 * blocks, wanted, -1)
    sign = jnp.where((swapped == 1) & (part == 1), -1.0, 1.0)
    place = jnp.where(iota((depth, 2 * LANES), 0) == wanted, sign, 0.0).astype(jnp.bfloat16)
    held[...] = (
        jnp.dot(x_ref[...].reshape(2 * rows, depth), place, preferred_element_type=jnp.float32)
        .astype(jnp.bfloat16)
        .reshape(2, rows, 2 * LANES)
    )
    right = held[:, :, 0:LANES].reshape(2 * rows, LANES)
    for q in range(2):
        product = lax.dot_general(
            held[pol, :, q * LANES : (q + 1) * LANES], right, (((1,), (1,)), ((), ())),
            preferred_element_type=jnp.float32,
        )
        out_ref[0, 0, q] = (product * (1.0 / blocks)).astype(jnp.bfloat16)


def fast_body(voltages, fir_taps, owner_map, station_flag_marks):
    stations, _, span, samples = voltages.shape
    taps = fir_taps.shape[0]
    blocks = span - taps + 1
    channels = owner_map.shape[0]
    tm_count = lax.axis_size("tm")
    owners = lax.axis_size("stn") * tm_count
    capacity = 2 * channels // owners
    steps = -(-span // STEP)
    lanes = blocks * 2 * capacity
    columns = taps * 2 * channels
    sizes = (stations, span, samples, taps, blocks, channels, owners, capacity, tm_count)
    vmem = pl.BlockSpec(memory_space=pltpu.VMEM)
    dma = pltpu.SemaphoreType.DMA
    x = pl.pallas_call(
        functools.partial(channelize_kernel, sizes),
        out_shape=jax.ShapeDtypeStruct((2, owners * stations, lanes), jnp.bfloat16),
        in_specs=[pl.BlockSpec(memory_space=pl.ANY), vmem, vmem, vmem, vmem],
        out_specs=vmem,
        scratch_shapes=[
            pltpu.VMEM((steps, stations, STEP, samples), jnp.bfloat16),
            pltpu.VMEM((stations, (span - 1) % STEP + 1, samples), jnp.bfloat16),
            pltpu.VMEM((samples, columns), jnp.bfloat16),
            pltpu.VMEM((columns // LANES, steps * stations * STEP, LANES), jnp.float32),
            pltpu.VMEM((owners, stations, lanes), jnp.bfloat16),
            dma((steps,)),
            dma((steps, owners)),
            dma((steps, owners)),
            dma((steps,)),
            dma((steps,)),
            dma((steps,)),
        ],
        compiler_params=pltpu.CompilerParams(
            collective_id=0, has_side_effects=True, vmem_limit_bytes=48 * 1024 * 1024
        ),
        name="channelize",
    )(
        voltages, fir_taps, jnp.asarray(wide_table(samples // 2, channels)), owner_map,
        station_flag_marks.reshape(1, stations),
    )
    rows = owners * stations
    return pl.pallas_call(
        functools.partial(correlate_kernel, blocks, capacity),
        grid=(capacity,),
        out_shape=jax.ShapeDtypeStruct((1, capacity, 2, rows, 2 * rows), jnp.bfloat16),
        in_specs=[pl.BlockSpec((2, rows, lanes), lambda k: (0, 0, 0))],
        out_specs=pl.BlockSpec((1, 1, 2, rows, 2 * rows), lambda k: (0, k, 0, 0, 0)),
        scratch_shapes=[pltpu.VMEM((2, rows, 2 * LANES), jnp.bfloat16)],
        compiler_params=pltpu.CompilerParams(vmem_limit_bytes=32 * 1024 * 1024),
        name="correlate",
    )(x)


def body(voltages, fir_taps, owner_map, station_flag_marks):
    stations, _, span, samples = voltages.shape
    taps = fir_taps.shape[0]
    channels = owner_map.shape[0]
    blocks = span - taps + 1
    owners = lax.axis_size("stn") * lax.axis_size("tm")
    width = 4 * channels // owners
    fits = (
        4 * channels == LANES
        and owners * width == LANES
        and GROUP * width == LANES
        and taps == GROUP
        and blocks % GROUP == 0
        and 2 * blocks <= LANES
        and stations % 16 == 0
        and samples % 512 == 0
        and lax.axis_size("pol") == 2
    )
    run = fast_body if fits else general_body
    return run(voltages, fir_taps, owner_map, station_flag_marks)


def solution(mesh):
    in_specs = (P(("group", "stn", "tm"), "pol", None, None), P(), P(), P(("stn", "tm")))
    out_specs = P(("group", "stn", "tm"), None, None, "pol", None)
    return jax.shard_map(body, mesh=mesh, in_specs=in_specs, out_specs=out_specs, check_vma=False)
```

```python
import functools
import math

import jax
import jax.numpy as jnp
import numpy as np
from jax import lax
from jax.experimental import pallas as pl
from jax.experimental.pallas import tpu as pltpu
from jax.sharding import PartitionSpec as P


def partner(value, axis, stride):
    return lax.ppermute(value, axis, [(i, i ^ 1 << stride) for i in range(lax.axis_size(axis))])


def dft_table(fft_length, channels):
    row_numbers = jnp.arange(fft_length, dtype=jnp.int32)[:, None]
    col_ids = jnp.arange(channels, dtype=jnp.int32)[None, :]
    phase_idx = (row_numbers * col_ids % fft_length).astype(jnp.float32) * (
        2.0 * math.pi / fft_length
    )
    norm_scale = 1.0 / math.sqrt(fft_length)
    cosine = (jnp.cos(phase_idx) * norm_scale).astype(jnp.bfloat16)
    sine_part = (jnp.sin(phase_idx) * norm_scale).astype(jnp.bfloat16)
    upper_rows = jnp.concatenate([cosine, -sine_part], axis=1)
    lower_rows = jnp.concatenate([sine_part, cosine], axis=1)
    return jnp.concatenate([upper_rows, lower_rows], axis=0)


def slot_matches(route_map, owners, capacity):
    channels = route_map.shape[0]
    position = jnp.arange(channels, dtype=jnp.int32)
    earlier = (route_map[:, None] == route_map[None, :]) & (position[None, :] < position[:, None])
    position_within_owner = jnp.sum(earlier.astype(jnp.int32), axis=1)
    owner_ids = jnp.arange(owners, dtype=jnp.int32)
    slot_ids = jnp.arange(capacity, dtype=jnp.int32)
    return (route_map[None, None, :] == owner_ids[:, None, None]) & (
        position_within_owner[None, None, :] == slot_ids[None, :, None]
    )


def corner_turn(outgoing):
    return lax.all_to_all(outgoing, ("stn", "tm"), split_axis=3, concat_axis=3, tiled=True)


def general_body(voltages, fir_taps, owner_map, station_flag_marks):
    st_dev = voltages.shape[0]
    span_blocks = voltages.shape[2]
    fft_length = voltages.shape[3] // 2
    tap_count = fir_taps.shape[0]
    blocks = span_blocks - tap_count + 1
    channels = owner_map.shape[0]
    stn_count = lax.axis_size("stn")
    tm_count = lax.axis_size("tm")
    owners = stn_count * tm_count
    capacity = 2 * channels // owners
    stations = st_dev * owners
    pol_index = lax.axis_index("pol")
    table = dft_table(fft_length, channels)
    wide_taps = jnp.concatenate([fir_taps, fir_taps], axis=1).astype(jnp.float32)
    samples = voltages[:, 0]
    filtered = wide_taps[0] * samples[:, 0:blocks].astype(jnp.float32)
    for tap_index in range(1, tap_count):
        filtered = filtered + wide_taps[tap_index] * samples[
            :, tap_index : tap_index + blocks
        ].astype(jnp.float32)
    flat_rows = filtered.astype(jnp.bfloat16).reshape(st_dev * blocks, 2 * fft_length)
    single_spectrum = jnp.dot(flat_rows, table, preferred_element_type=jnp.float32).reshape(
        st_dev, blocks, 2, channels
    )
    clean_stations = (1 - station_flag_marks).astype(jnp.float32)
    channel_spectra = (single_spectrum * clean_stations[:, None, None, None]).astype(jnp.bfloat16)
    pick_matrix = slot_matches(owner_map[:, 0], owners, capacity).astype(jnp.bfloat16)
    outgoing = jnp.einsum(
        "okc,sbqc->kqosb", pick_matrix, channel_spectra, preferred_element_type=jnp.float32
    )
    outgoing = outgoing.astype(jnp.bfloat16).reshape(capacity, 2, 1, owners, st_dev * blocks)
    arrived = corner_turn(outgoing)
    row_block = arrived.reshape(capacity, 2, stations, blocks)
    other_block = partner(row_block, "pol", 0)
    col_block = jnp.where(
        pol_index == 0,
        jnp.concatenate([row_block, other_block], axis=2),
        jnp.concatenate([other_block, row_block], axis=2),
    )
    products = jnp.einsum(
        "kqib,krjb->kqrij", row_block, col_block, preferred_element_type=jnp.float32
    )
    real_part = (products[:, 0, 0] + products[:, 1, 1]) / blocks
    imag_part = (products[:, 1, 0] - products[:, 0, 1]) / blocks
    return jnp.stack([real_part, imag_part], axis=1).astype(jnp.bfloat16)[None]


GROUP = 8
LANES = 128


def wide_table(fft_length, channels):
    n = np.arange(fft_length, dtype=np.int64)[:, None]
    k = np.arange(channels, dtype=np.int64)[None, :]
    phase = (n * k % fft_length).astype(np.float32) * np.float32(2.0 * math.pi / fft_length)
    scale = np.float32(1.0 / math.sqrt(fft_length))
    cosine = (np.cos(phase) * scale).astype(jnp.bfloat16)
    sine = (np.sin(phase) * scale).astype(jnp.bfloat16)
    upper = np.concatenate([cosine, -sine], axis=1)
    lower = np.concatenate([sine, cosine], axis=1)
    whole = np.concatenate([upper, lower], axis=0)
    return np.concatenate([whole] * (LANES // (2 * channels)), axis=1)


def row_cuts(groups):
    return [0] + list(range(1, groups, 2)) + [groups]


def iota(shape, dim):
    return lax.broadcasted_iota(jnp.int32, shape, dim)


def slot_columns(owner_ref, channels, capacity):
    square = iota((channels, channels), 0) == iota((channels, channels), 1)
    col = jnp.sum(jnp.where(square, owner_ref[...], 0), axis=1, keepdims=True)
    lane = iota((channels, LANES), 1)
    channel = lane % channels
    row_number = iota((channels, LANES), 0)
    owner = jnp.sum(jnp.where(row_number == channel, col, 0), axis=0, keepdims=True)
    rank = jnp.sum(
        jnp.where((col == owner) & (row_number < channel), 1, 0), axis=0, keepdims=True
    )
    lane = iota((1, LANES), 1)
    place = (owner * capacity + rank) * 2 + lane // channels
    place = jnp.where(lane < 2 * channels, place, -1)
    hot = jnp.where(iota((LANES, LANES), 0) == place, 1.0, 0.0)
    return hot.T.astype(jnp.bfloat16)


def block_transpose(parts, width):
    count = len(parts)
    lane = iota(parts[0].shape, 1) // width
    half = 1
    while half < count:
        low = lane // half % 2 == 0
        out = list(parts)
        for i in range(count):
            if i // half % 2 == 0:
                a, b = parts[i], parts[i + half]
                out[i] = jnp.where(low, a, pltpu.roll(b, half * width, 1))
                out[i + half] = jnp.where(low, pltpu.roll(a, LANES - half * width, 1), b)
        parts = out
        half *= 2
    return parts


def channelize_kernel(
    sizes, v_ref, taps_ref, table_ref, owner_ref, marks_ref, x_ref,
    vbuf, wbuf, zbuf, sendbuf, in_sem, send_sem, recv_sem, own_sem, pass_send, pass_recv,
):
    stations, span, samples, taps, blocks, channels, owners, capacity, tm_count = sizes
    cuts = row_cuts(blocks // GROUP)
    steps = len(cuts) - 1
    width = 2 * capacity
    pol = lax.axis_index("pol")
    me = lax.axis_index("stn") * tm_count + lax.axis_index("tm")
    ends = [0] + [cut * GROUP + taps - 1 for cut in cuts[1:]]

    loads = []
    for c in range(steps):
        rows = pl.ds(ends[c], ends[c + 1] - ends[c])
        load = pltpu.make_async_copy(v_ref.at[rows], vbuf.at[rows], in_sem.at[c])
        load.start()
        loads.append(load)

    barrier = pltpu.get_barrier_semaphore()
    for k in range(1, owners):
        peer = lax.rem(me + k, owners)
        pl.semaphore_signal(
            barrier, inc=1, device_id={"stn": peer // tm_count, "tm": lax.rem(peer, tm_count)},
            device_id_type=pl.DeviceIdType.MESH,
        )
    pl.semaphore_signal(
        barrier, inc=1, device_id={"pol": 1 - pol}, device_id_type=pl.DeviceIdType.MESH
    )

    columns = taps * 2 * channels
    expand = jnp.where(
        iota((taps, columns), 0) == iota((taps, columns), 1) // (2 * channels), 1.0, 0.0
    ).astype(jnp.bfloat16)
    half = samples // 2
    piece = 256
    for i in range(half // piece):
        tap_rows = lax.dot_general(
            taps_ref[:, i * piece : (i + 1) * piece], expand,
            (((0,), (0,)), ((), ())), preferred_element_type=jnp.float32,
        )
        for base in (0, half):
            at = slice(base + i * piece, base + (i + 1) * piece)
            entry = table_ref[at, :].astype(jnp.float32)
            for j in range(columns // LANES):
                lanes = slice(j * LANES, (j + 1) * LANES)
                wbuf[at, lanes] = (tap_rows[:, lanes] * entry).astype(jnp.bfloat16)

    pick = slot_columns(owner_ref, channels, capacity)
    diagonal = iota((stations, stations), 0) == iota((stations, stations), 1)
    keep = 1.0 - jnp.sum(
        jnp.where(diagonal, marks_ref[...], 0), axis=1, keepdims=True
    ).astype(jnp.float32)
    pl.semaphore_wait(barrier, owners)

    def shifted(b):
        total = None
        for j in range(columns // LANES):
            row = b + 2 * j
            term = zbuf[row * stations : (row + 1) * stations, j * LANES : (j + 1) * LANES]
            total = term if total is None else total + term
        return total

    sends, passes = [], []

    def send_groups(c, first, last):
        lanes = pl.ds(first * LANES, (last - first) * LANES)
        rows = pl.ds(me * stations, stations)
        for g in range(first, last):
            summed = [shifted(g * GROUP + i) for i in range(GROUP + 1)]
            spectra = [
                ((summed[i] + pltpu.roll(summed[i + 1], 2 * channels, 1)) * keep).astype(jnp.bfloat16)
                for i in range(GROUP)
            ]
            placed = jnp.dot(
                jnp.concatenate(spectra, axis=0), pick, preferred_element_type=jnp.float32
            )
            parts = [placed[i * stations : (i + 1) * stations] for i in range(GROUP)]
            for o, part in enumerate(block_transpose(parts, width)):
                sendbuf[o, :, g * LANES : (g + 1) * LANES] = part.astype(jnp.bfloat16)
        batch = []
        for k in range(1, owners):
            peer = lax.rem(me + k, owners)
            copy = pltpu.make_async_remote_copy(
                src_ref=sendbuf.at[peer, :, lanes],
                dst_ref=x_ref.at[pol, rows, lanes],
                send_sem=send_sem.at[c, k],
                recv_sem=recv_sem.at[c, k],
                device_id={"stn": peer // tm_count, "tm": lax.rem(peer, tm_count)},
                device_id_type=pl.DeviceIdType.MESH,
            )
            copy.start()
            batch.append(copy)
        own = pltpu.make_async_copy(
            sendbuf.at[me, :, lanes], x_ref.at[pol, rows, lanes], own_sem.at[c]
        )
        own.start()
        sends.append((batch, own, lanes))

    def pass_on(c):
        batch, own, lanes = sends[c]
        own.wait()
        for k in range(1, owners):
            source = lax.rem(me + owners - k, owners)
            here = x_ref.at[pol, pl.ds(source * stations, stations), lanes]
            pltpu.make_async_copy(here, here, recv_sem.at[c, k]).wait()
        mine = x_ref.at[pol, :, lanes]
        copy = pltpu.make_async_remote_copy(
            src_ref=mine, dst_ref=mine, send_sem=pass_send.at[c], recv_sem=pass_recv.at[c],
            device_id={"pol": 1 - pol}, device_id_type=pl.DeviceIdType.MESH,
        )
        copy.start()
        passes.append(copy)

    for c in range(steps):
        loads[c].wait()
        first, last = ends[c], ends[c + 1]
        zbuf[first * stations : last * stations, :] = jnp.dot(
            vbuf[first:last].reshape((last - first) * stations, samples), wbuf[...],
            preferred_element_type=jnp.float32,
        )
        if c >= 1:
            pass_on(c - 1)
        send_groups(c, cuts[c], cuts[c + 1])
    pass_on(steps - 1)
    for batch, own, lanes in sends:
        for copy in batch:
            copy.wait_send()
    for copy in passes:
        copy.wait()


def lane_places(blocks, capacity):
    table = np.zeros((blocks, capacity, 2, capacity, 2, LANES // 2), np.float32)
    for k in range(capacity):
        for q in range(2):
            table[np.arange(blocks), k, q, k, q, np.arange(blocks)] = 1.0
    return table.reshape(blocks * capacity * 2, capacity * LANES).astype(jnp.bfloat16)


def correlate_kernel(blocks, capacity, x_ref, place_ref, out_ref, held, result, out_sem):
    pol = lax.axis_index("pol")
    rows, depth = x_ref.shape[1], x_ref.shape[2]
    signal = x_ref[...].reshape(2 * rows, depth)
    sign = jnp.where(iota((1, LANES), 1) < LANES // 2, 1.0, -1.0)
    copies = []
    for pair in range(capacity // 2):
        lanes = slice(pair * 2 * LANES, (pair + 1) * 2 * LANES)
        held[:, :, lanes] = (
            jnp.dot(signal, place_ref[:, lanes], preferred_element_type=jnp.float32)
            .astype(jnp.bfloat16)
            .reshape(2, rows, 2 * LANES)
        )
        for k in (2 * pair, 2 * pair + 1):
            lanes = slice(k * LANES, (k + 1) * LANES)
            right = held[:, :, lanes].reshape(2 * rows, LANES)
            left = held[pol, :, lanes]
            turned = pltpu.roll(left.astype(jnp.float32), LANES // 2, 1) * sign
            for q, operand in enumerate((left, turned.astype(jnp.bfloat16))):
                product = lax.dot_general(
                    operand, right, (((1,), (1,)), ((), ())), preferred_element_type=jnp.float32
                )
                result[k, q] = (product * (1.0 / blocks)).astype(jnp.bfloat16)
            copy = pltpu.make_async_copy(result.at[k], out_ref.at[0, k], out_sem.at[k])
            copy.start()
            copies.append(copy)
    for copy in copies:
        copy.wait()


def fast_body(voltages, fir_taps, owner_map, station_flag_marks):
    stations, _, span, samples = voltages.shape
    taps = fir_taps.shape[0]
    blocks = span - taps + 1
    channels = owner_map.shape[0]
    tm_count = lax.axis_size("tm")
    owners = lax.axis_size("stn") * tm_count
    capacity = 2 * channels // owners
    steps = len(row_cuts(blocks // GROUP)) - 1
    lanes = blocks * 2 * capacity
    columns = taps * 2 * channels
    sizes = (stations, span, samples, taps, blocks, channels, owners, capacity, tm_count)
    vmem = pl.BlockSpec(memory_space=pltpu.VMEM)
    dma = pltpu.SemaphoreType.DMA
    x = pl.pallas_call(
        functools.partial(channelize_kernel, sizes),
        out_shape=jax.ShapeDtypeStruct((2, owners * stations, lanes), jnp.bfloat16),
        in_specs=[pl.BlockSpec(memory_space=pl.ANY), vmem, vmem, vmem, vmem],
        out_specs=vmem,
        scratch_shapes=[
            pltpu.VMEM((span, stations, samples), jnp.bfloat16),
            pltpu.VMEM((samples, columns), jnp.bfloat16),
            pltpu.VMEM((span * stations, columns), jnp.float32),
            pltpu.VMEM((owners, stations, lanes), jnp.bfloat16),
            dma((steps,)),
            dma((steps, owners)),
            dma((steps, owners)),
            dma((steps,)),
            dma((steps,)),
            dma((steps,)),
        ],
        compiler_params=pltpu.CompilerParams(
            collective_id=0, has_side_effects=True, vmem_limit_bytes=52 * 1024 * 1024
        ),
        name="channelize",
    )(
        jnp.transpose(voltages[:, 0], (1, 0, 2)), fir_taps, jnp.asarray(wide_table(samples // 2, channels)),
        owner_map.reshape(1, channels),
        station_flag_marks.reshape(1, stations),
    )
    rows = owners * stations
    return pl.pallas_call(
        functools.partial(correlate_kernel, blocks, capacity),
        out_shape=jax.ShapeDtypeStruct((1, capacity, 2, rows, 2 * rows), jnp.bfloat16),
        in_specs=[vmem, vmem],
        out_specs=pl.BlockSpec(memory_space=pl.ANY),
        scratch_shapes=[
            pltpu.VMEM((2, rows, capacity * LANES), jnp.bfloat16),
            pltpu.VMEM((capacity, 2, rows, 2 * rows), jnp.bfloat16),
            dma((capacity,)),
        ],
        compiler_params=pltpu.CompilerParams(vmem_limit_bytes=24 * 1024 * 1024),
        name="correlate",
    )(x, jnp.asarray(lane_places(blocks, capacity)))


def body(voltages, fir_taps, owner_map, station_flag_marks):
    stations, _, span, samples = voltages.shape
    taps = fir_taps.shape[0]
    channels = owner_map.shape[0]
    blocks = span - taps + 1
    owners = lax.axis_size("stn") * lax.axis_size("tm")
    width = 4 * channels // owners
    fits = (
        4 * channels == LANES
        and owners * width == LANES
        and GROUP * width == LANES
        and taps == GROUP
        and blocks % GROUP == 0
        and blocks <= LANES // 2
        and width % 4 == 0
        and stations % 16 == 0
        and samples % 512 == 0
        and lax.axis_size("pol") == 2
    )
    run = fast_body if fits else general_body
    return run(voltages, fir_taps, owner_map, station_flag_marks)


def solution(mesh):
    in_specs = (P(("group", "stn", "tm"), "pol", None, None), P(), P(), P(("stn", "tm")))
    out_specs = P(("group", "stn", "tm"), None, None, "pol", None)
    return jax.shard_map(body, mesh=mesh, in_specs=in_specs, out_specs=out_specs, check_vma=False)
```

```python
import functools
import math

import jax
import jax.numpy as jnp
import numpy as np
from jax import lax
from jax.experimental import pallas as pl
from jax.experimental.pallas import tpu as pltpu
from jax.sharding import PartitionSpec as P


def partner(value, axis, stride):
    return lax.ppermute(value, axis, [(i, i ^ 1 << stride) for i in range(lax.axis_size(axis))])


def dft_table(fft_length, channels):
    row_numbers = jnp.arange(fft_length, dtype=jnp.int32)[:, None]
    col_ids = jnp.arange(channels, dtype=jnp.int32)[None, :]
    phase_idx = (row_numbers * col_ids % fft_length).astype(jnp.float32) * (
        2.0 * math.pi / fft_length
    )
    norm_scale = 1.0 / math.sqrt(fft_length)
    cosine = (jnp.cos(phase_idx) * norm_scale).astype(jnp.bfloat16)
    sine_part = (jnp.sin(phase_idx) * norm_scale).astype(jnp.bfloat16)
    upper_rows = jnp.concatenate([cosine, -sine_part], axis=1)
    lower_rows = jnp.concatenate([sine_part, cosine], axis=1)
    return jnp.concatenate([upper_rows, lower_rows], axis=0)


def slot_matches(route_map, owners, capacity):
    channels = route_map.shape[0]
    position = jnp.arange(channels, dtype=jnp.int32)
    earlier = (route_map[:, None] == route_map[None, :]) & (position[None, :] < position[:, None])
    position_within_owner = jnp.sum(earlier.astype(jnp.int32), axis=1)
    owner_ids = jnp.arange(owners, dtype=jnp.int32)
    slot_ids = jnp.arange(capacity, dtype=jnp.int32)
    return (route_map[None, None, :] == owner_ids[:, None, None]) & (
        position_within_owner[None, None, :] == slot_ids[None, :, None]
    )


def corner_turn(outgoing):
    return lax.all_to_all(outgoing, ("stn", "tm"), split_axis=3, concat_axis=3, tiled=True)


def general_body(voltages, fir_taps, owner_map, station_flag_marks):
    st_dev = voltages.shape[0]
    span_blocks = voltages.shape[2]
    fft_length = voltages.shape[3] // 2
    tap_count = fir_taps.shape[0]
    blocks = span_blocks - tap_count + 1
    channels = owner_map.shape[0]
    stn_count = lax.axis_size("stn")
    tm_count = lax.axis_size("tm")
    owners = stn_count * tm_count
    capacity = 2 * channels // owners
    stations = st_dev * owners
    pol_index = lax.axis_index("pol")
    table = dft_table(fft_length, channels)
    wide_taps = jnp.concatenate([fir_taps, fir_taps], axis=1).astype(jnp.float32)
    samples = voltages[:, 0]
    filtered = wide_taps[0] * samples[:, 0:blocks].astype(jnp.float32)
    for tap_index in range(1, tap_count):
        filtered = filtered + wide_taps[tap_index] * samples[
            :, tap_index : tap_index + blocks
        ].astype(jnp.float32)
    flat_rows = filtered.astype(jnp.bfloat16).reshape(st_dev * blocks, 2 * fft_length)
    single_spectrum = jnp.dot(flat_rows, table, preferred_element_type=jnp.float32).reshape(
        st_dev, blocks, 2, channels
    )
    clean_stations = (1 - station_flag_marks).astype(jnp.float32)
    channel_spectra = (single_spectrum * clean_stations[:, None, None, None]).astype(jnp.bfloat16)
    pick_matrix = slot_matches(owner_map[:, 0], owners, capacity).astype(jnp.bfloat16)
    outgoing = jnp.einsum(
        "okc,sbqc->kqosb", pick_matrix, channel_spectra, preferred_element_type=jnp.float32
    )
    outgoing = outgoing.astype(jnp.bfloat16).reshape(capacity, 2, 1, owners, st_dev * blocks)
    arrived = corner_turn(outgoing)
    row_block = arrived.reshape(capacity, 2, stations, blocks)
    other_block = partner(row_block, "pol", 0)
    col_block = jnp.where(
        pol_index == 0,
        jnp.concatenate([row_block, other_block], axis=2),
        jnp.concatenate([other_block, row_block], axis=2),
    )
    products = jnp.einsum(
        "kqib,krjb->kqrij", row_block, col_block, preferred_element_type=jnp.float32
    )
    real_part = (products[:, 0, 0] + products[:, 1, 1]) / blocks
    imag_part = (products[:, 1, 0] - products[:, 0, 1]) / blocks
    return jnp.stack([real_part, imag_part], axis=1).astype(jnp.bfloat16)[None]


GROUP = 8
LANES = 128


def wide_table(fft_length, channels):
    n = np.arange(fft_length, dtype=np.int64)[:, None]
    k = np.arange(channels, dtype=np.int64)[None, :]
    phase = (n * k % fft_length).astype(np.float32) * np.float32(2.0 * math.pi / fft_length)
    scale = np.float32(1.0 / math.sqrt(fft_length))
    cosine = (np.cos(phase) * scale).astype(jnp.bfloat16)
    sine = (np.sin(phase) * scale).astype(jnp.bfloat16)
    upper = np.concatenate([cosine, -sine], axis=1)
    lower = np.concatenate([sine, cosine], axis=1)
    whole = np.concatenate([upper, lower], axis=0)
    return np.concatenate([whole] * (LANES // (2 * channels)), axis=1)


def row_cuts(groups):
    return [0] + list(range(1, groups, 2)) + [groups]


def iota(shape, dim):
    return lax.broadcasted_iota(jnp.int32, shape, dim)


def slot_columns(owner_ref, channels, capacity):
    square = iota((channels, channels), 0) == iota((channels, channels), 1)
    col = jnp.sum(jnp.where(square, owner_ref[...], 0), axis=1, keepdims=True)
    lane = iota((channels, LANES), 1)
    channel = lane % channels
    row_number = iota((channels, LANES), 0)
    owner = jnp.sum(jnp.where(row_number == channel, col, 0), axis=0, keepdims=True)
    rank = jnp.sum(
        jnp.where((col == owner) & (row_number < channel), 1, 0), axis=0, keepdims=True
    )
    lane = iota((1, LANES), 1)
    place = (owner * capacity + rank) * 2 + lane // channels
    place = jnp.where(lane < 2 * channels, place, -1)
    hot = jnp.where(iota((LANES, LANES), 0) == place, 1.0, 0.0)
    return hot.T.astype(jnp.bfloat16)


def block_transpose(parts, width):
    count = len(parts)
    lane = iota(parts[0].shape, 1) // width
    half = 1
    while half < count:
        low = lane // half % 2 == 0
        out = list(parts)
        for i in range(count):
            if i // half % 2 == 0:
                a, b = parts[i], parts[i + half]
                out[i] = jnp.where(low, a, pltpu.roll(b, half * width, 1))
                out[i + half] = jnp.where(low, pltpu.roll(a, LANES - half * width, 1), b)
        parts = out
        half *= 2
    return parts


def channelize_kernel(
    sizes, v_ref, taps_hbm, table_hbm, owner_hbm, marks_hbm, x_ref,
    taps_ref, table_ref, owner_ref, marks_ref, small_sem, vbuf, wbuf, zbuf, sendbuf, in_sem, send_sem, recv_sem, own_sem, pass_send, pass_recv,
):
    stations, span, samples, taps, blocks, channels, owners, capacity, tm_count = sizes
    cuts = row_cuts(blocks // GROUP)
    steps = len(cuts) - 1
    width = 2 * capacity
    pol = lax.axis_index("pol")
    me = lax.axis_index("stn") * tm_count + lax.axis_index("tm")
    ends = [0] + [cut * GROUP + taps - 1 for cut in cuts[1:]]

    small = [
        pltpu.make_async_copy(source, target, small_sem.at[i])
        for i, (source, target) in enumerate((
            (taps_hbm, taps_ref), (table_hbm, table_ref), (owner_hbm, owner_ref),
            (marks_hbm, marks_ref),
        ))
    ]
    for load in small:
        load.start()
    loads = []
    for c in range(steps):
        rows = pl.ds(ends[c], ends[c + 1] - ends[c])
        load = pltpu.make_async_copy(v_ref.at[rows], vbuf.at[rows], in_sem.at[c])
        load.start()
        loads.append(load)

    barrier = pltpu.get_barrier_semaphore()
    for k in range(1, owners):
        peer = lax.rem(me + k, owners)
        pl.semaphore_signal(
            barrier, inc=1, device_id={"stn": peer // tm_count, "tm": lax.rem(peer, tm_count)},
            device_id_type=pl.DeviceIdType.MESH,
        )
    pl.semaphore_signal(
        barrier, inc=1, device_id={"pol": 1 - pol}, device_id_type=pl.DeviceIdType.MESH
    )

    for load in small:
        load.wait()
    columns = taps * 2 * channels
    expand = jnp.where(
        iota((taps, columns), 0) == iota((taps, columns), 1) // (2 * channels), 1.0, 0.0
    ).astype(jnp.bfloat16)
    half = samples // 2
    piece = 256
    for i in range(half // piece):
        tap_rows = lax.dot_general(
            taps_ref[:, i * piece : (i + 1) * piece], expand,
            (((0,), (0,)), ((), ())), preferred_element_type=jnp.float32,
        )
        for base in (0, half):
            at = slice(base + i * piece, base + (i + 1) * piece)
            entry = table_ref[at, :].astype(jnp.float32)
            for j in range(columns // LANES):
                lanes = slice(j * LANES, (j + 1) * LANES)
                wbuf[at, lanes] = (tap_rows[:, lanes] * entry).astype(jnp.bfloat16)

    pick = slot_columns(owner_ref, channels, capacity)
    diagonal = iota((stations, stations), 0) == iota((stations, stations), 1)
    keep = 1.0 - jnp.sum(
        jnp.where(diagonal, marks_ref[...], 0), axis=1, keepdims=True
    ).astype(jnp.float32)
    pl.semaphore_wait(barrier, owners)

    def shifted(b):
        total = None
        for j in range(columns // LANES):
            row = b + 2 * j
            term = zbuf[row * stations : (row + 1) * stations, j * LANES : (j + 1) * LANES]
            total = term if total is None else total + term
        return total

    sends, passes = [], []

    def send_groups(c, first, last):
        batch_groups = pl.ds(first, last - first)
        for g in range(first, last):
            summed = [shifted(g * GROUP + i) for i in range(GROUP + 1)]
            spectra = [
                ((summed[i] + pltpu.roll(summed[i + 1], 2 * channels, 1)) * keep).astype(jnp.bfloat16)
                for i in range(GROUP)
            ]
            placed = jnp.dot(
                jnp.concatenate(spectra, axis=0), pick, preferred_element_type=jnp.float32
            )
            parts = [placed[i * stations : (i + 1) * stations] for i in range(GROUP)]
            for o, part in enumerate(block_transpose(parts, width)):
                sendbuf[o, g] = part.astype(jnp.bfloat16)
        batch = []
        for k in range(1, owners):
            peer = lax.rem(me + k, owners)
            copy = pltpu.make_async_remote_copy(
                src_ref=sendbuf.at[peer, batch_groups],
                dst_ref=x_ref.at[pol, me, batch_groups],
                send_sem=send_sem.at[c, k],
                recv_sem=recv_sem.at[c, k],
                device_id={"stn": peer // tm_count, "tm": lax.rem(peer, tm_count)},
                device_id_type=pl.DeviceIdType.MESH,
            )
            copy.start()
            batch.append(copy)
        own = pltpu.make_async_copy(
            sendbuf.at[me, batch_groups], x_ref.at[pol, me, batch_groups], own_sem.at[c]
        )
        own.start()
        sends.append((batch, own, batch_groups))

    def pass_on(c):
        batch, own, batch_groups = sends[c]
        own.wait()
        for k in range(1, owners):
            source = lax.rem(me + owners - k, owners)
            here = x_ref.at[pol, source, batch_groups]
            pltpu.make_async_copy(here, here, recv_sem.at[c, k]).wait()
        mine = x_ref.at[pol, :, batch_groups]
        copy = pltpu.make_async_remote_copy(
            src_ref=mine, dst_ref=mine, send_sem=pass_send.at[c], recv_sem=pass_recv.at[c],
            device_id={"pol": 1 - pol}, device_id_type=pl.DeviceIdType.MESH,
        )
        copy.start()
        passes.append(copy)

    for c in range(steps):
        loads[c].wait()
        first, last = ends[c], ends[c + 1]
        zbuf[first * stations : last * stations, :] = jnp.dot(
            vbuf[first:last].reshape((last - first) * stations, samples), wbuf[...],
            preferred_element_type=jnp.float32,
        )
        send_groups(c, cuts[c], cuts[c + 1])
    for c in range(steps):
        pass_on(c)
    for batch, own, batch_groups in sends:
        for copy in batch:
            copy.wait_send()
    for copy in passes:
        copy.wait()


def lane_places(blocks, capacity):
    table = np.zeros((blocks, capacity, 2, capacity, 2, LANES // 2), np.float32)
    for k in range(capacity):
        for q in range(2):
            table[np.arange(blocks), k, q, k, q, np.arange(blocks)] = 1.0
    return table.reshape(blocks * capacity * 2, capacity * LANES).astype(jnp.bfloat16)


def correlate_kernel(blocks, capacity, x_ref, place_ref, out_ref, held, result, out_sem):
    pol = lax.axis_index("pol")
    _, owners, groups, stations, _ = x_ref.shape
    rows = owners * stations
    signal = jnp.concatenate(
        [x_ref[:, :, g].reshape(2 * rows, LANES) for g in range(groups)], axis=1
    )
    sign = jnp.where(iota((1, LANES), 1) < LANES // 2, 1.0, -1.0)
    copies = []
    for pair in range(capacity // 2):
        lanes = slice(pair * 2 * LANES, (pair + 1) * 2 * LANES)
        held[:, :, lanes] = (
            jnp.dot(signal, place_ref[:, lanes], preferred_element_type=jnp.float32)
            .astype(jnp.bfloat16)
            .reshape(2, rows, 2 * LANES)
        )
        for k in (2 * pair, 2 * pair + 1):
            lanes = slice(k * LANES, (k + 1) * LANES)
            right = held[:, :, lanes].reshape(2 * rows, LANES)
            left = held[pol, :, lanes]
            turned = pltpu.roll(left.astype(jnp.float32), LANES // 2, 1) * sign
            for q, operand in enumerate((left, turned.astype(jnp.bfloat16))):
                product = lax.dot_general(
                    operand, right, (((1,), (1,)), ((), ())), preferred_element_type=jnp.float32
                )
                result[k, q] = (product * (1.0 / blocks)).astype(jnp.bfloat16)
            copy = pltpu.make_async_copy(result.at[k], out_ref.at[0, k], out_sem.at[k])
            copy.start()
            copies.append(copy)
    for copy in copies:
        copy.wait()


def fast_body(voltages, fir_taps, owner_map, station_flag_marks):
    stations, _, span, samples = voltages.shape
    taps = fir_taps.shape[0]
    blocks = span - taps + 1
    channels = owner_map.shape[0]
    tm_count = lax.axis_size("tm")
    owners = lax.axis_size("stn") * tm_count
    capacity = 2 * channels // owners
    groups = blocks // GROUP
    steps = len(row_cuts(groups)) - 1
    columns = taps * 2 * channels
    sizes = (stations, span, samples, taps, blocks, channels, owners, capacity, tm_count)
    vmem = pl.BlockSpec(memory_space=pltpu.VMEM)
    dma = pltpu.SemaphoreType.DMA
    x = pl.pallas_call(
        functools.partial(channelize_kernel, sizes),
        out_shape=jax.ShapeDtypeStruct((2, owners, groups, stations, LANES), jnp.bfloat16),
        in_specs=[pl.BlockSpec(memory_space=pltpu.HBM)] * 5,
        out_specs=vmem,
        scratch_shapes=[
            pltpu.VMEM(fir_taps.shape, jnp.bfloat16),
            pltpu.VMEM((samples, LANES), jnp.bfloat16),
            pltpu.VMEM((1, channels), jnp.int32),
            pltpu.VMEM((1, stations), jnp.int32),
            dma((4,)),
            pltpu.VMEM((span, stations, samples), jnp.bfloat16),
            pltpu.VMEM((samples, columns), jnp.bfloat16),
            pltpu.VMEM((span * stations, columns), jnp.float32),
            pltpu.VMEM((owners, groups, stations, LANES), jnp.bfloat16),
            dma((steps,)),
            dma((steps, owners)),
            dma((steps, owners)),
            dma((steps,)),
            dma((steps,)),
            dma((steps,)),
        ],
        compiler_params=pltpu.CompilerParams(
            collective_id=0, has_side_effects=True, vmem_limit_bytes=48 * 1024 * 1024
        ),
        name="channelize",
    )(
        jnp.transpose(voltages[:, 0], (1, 0, 2)), fir_taps, jnp.asarray(wide_table(samples // 2, channels)),
        owner_map.reshape(1, channels),
        station_flag_marks.reshape(1, stations),
    )
    rows = owners * stations
    return pl.pallas_call(
        functools.partial(correlate_kernel, blocks, capacity),
        out_shape=jax.ShapeDtypeStruct((1, capacity, 2, rows, 2 * rows), jnp.bfloat16),
        in_specs=[vmem, vmem],
        out_specs=pl.BlockSpec(memory_space=pl.ANY),
        scratch_shapes=[
            pltpu.VMEM((2, rows, capacity * LANES), jnp.bfloat16),
            pltpu.VMEM((capacity, 2, rows, 2 * rows), jnp.bfloat16),
            dma((capacity,)),
        ],
        compiler_params=pltpu.CompilerParams(vmem_limit_bytes=24 * 1024 * 1024),
        name="correlate",
    )(x, jnp.asarray(lane_places(blocks, capacity)))


def body(voltages, fir_taps, owner_map, station_flag_marks):
    stations, _, span, samples = voltages.shape
    taps = fir_taps.shape[0]
    channels = owner_map.shape[0]
    blocks = span - taps + 1
    owners = lax.axis_size("stn") * lax.axis_size("tm")
    width = 4 * channels // owners
    fits = (
        4 * channels == LANES
        and owners * width == LANES
        and GROUP * width == LANES
        and taps == GROUP
        and blocks % GROUP == 0
        and blocks <= LANES // 2
        and width % 4 == 0
        and stations % 16 == 0
        and samples % 512 == 0
        and lax.axis_size("pol") == 2
    )
    run = fast_body if fits else general_body
    return run(voltages, fir_taps, owner_map, station_flag_marks)


def solution(mesh):
    in_specs = (P(("group", "stn", "tm"), "pol", None, None), P(), P(), P(("stn", "tm")))
    out_specs = P(("group", "stn", "tm"), None, None, "pol", None)
    return jax.shard_map(body, mesh=mesh, in_specs=in_specs, out_specs=out_specs, check_vma=False)
```

```python
import functools
import math

import jax
import jax.numpy as jnp
import numpy as np
from jax import lax
from jax.experimental import pallas as pl
from jax.experimental.pallas import tpu as pltpu
from jax.sharding import PartitionSpec as P


def partner(value, axis, stride):
    return lax.ppermute(value, axis, [(i, i ^ 1 << stride) for i in range(lax.axis_size(axis))])


def dft_table(fft_length, channels):
    row_numbers = jnp.arange(fft_length, dtype=jnp.int32)[:, None]
    col_ids = jnp.arange(channels, dtype=jnp.int32)[None, :]
    phase_idx = (row_numbers * col_ids % fft_length).astype(jnp.float32) * (
        2.0 * math.pi / fft_length
    )
    norm_scale = 1.0 / math.sqrt(fft_length)
    cosine = (jnp.cos(phase_idx) * norm_scale).astype(jnp.bfloat16)
    sine_part = (jnp.sin(phase_idx) * norm_scale).astype(jnp.bfloat16)
    upper_rows = jnp.concatenate([cosine, -sine_part], axis=1)
    lower_rows = jnp.concatenate([sine_part, cosine], axis=1)
    return jnp.concatenate([upper_rows, lower_rows], axis=0)


def slot_matches(route_map, owners, capacity):
    channels = route_map.shape[0]
    position = jnp.arange(channels, dtype=jnp.int32)
    earlier = (route_map[:, None] == route_map[None, :]) & (position[None, :] < position[:, None])
    position_within_owner = jnp.sum(earlier.astype(jnp.int32), axis=1)
    owner_ids = jnp.arange(owners, dtype=jnp.int32)
    slot_ids = jnp.arange(capacity, dtype=jnp.int32)
    return (route_map[None, None, :] == owner_ids[:, None, None]) & (
        position_within_owner[None, None, :] == slot_ids[None, :, None]
    )


def corner_turn(outgoing):
    return lax.all_to_all(outgoing, ("stn", "tm"), split_axis=3, concat_axis=3, tiled=True)


def general_body(voltages, fir_taps, owner_map, station_flag_marks):
    st_dev = voltages.shape[0]
    span_blocks = voltages.shape[2]
    fft_length = voltages.shape[3] // 2
    tap_count = fir_taps.shape[0]
    blocks = span_blocks - tap_count + 1
    channels = owner_map.shape[0]
    stn_count = lax.axis_size("stn")
    tm_count = lax.axis_size("tm")
    owners = stn_count * tm_count
    capacity = 2 * channels // owners
    stations = st_dev * owners
    pol_index = lax.axis_index("pol")
    table = dft_table(fft_length, channels)
    wide_taps = jnp.concatenate([fir_taps, fir_taps], axis=1).astype(jnp.float32)
    samples = voltages[:, 0]
    filtered = wide_taps[0] * samples[:, 0:blocks].astype(jnp.float32)
    for tap_index in range(1, tap_count):
        filtered = filtered + wide_taps[tap_index] * samples[
            :, tap_index : tap_index + blocks
        ].astype(jnp.float32)
    flat_rows = filtered.astype(jnp.bfloat16).reshape(st_dev * blocks, 2 * fft_length)
    single_spectrum = jnp.dot(flat_rows, table, preferred_element_type=jnp.float32).reshape(
        st_dev, blocks, 2, channels
    )
    clean_stations = (1 - station_flag_marks).astype(jnp.float32)
    channel_spectra = (single_spectrum * clean_stations[:, None, None, None]).astype(jnp.bfloat16)
    pick_matrix = slot_matches(owner_map[:, 0], owners, capacity).astype(jnp.bfloat16)
    outgoing = jnp.einsum(
        "okc,sbqc->kqosb", pick_matrix, channel_spectra, preferred_element_type=jnp.float32
    )
    outgoing = outgoing.astype(jnp.bfloat16).reshape(capacity, 2, 1, owners, st_dev * blocks)
    arrived = corner_turn(outgoing)
    row_block = arrived.reshape(capacity, 2, stations, blocks)
    other_block = partner(row_block, "pol", 0)
    col_block = jnp.where(
        pol_index == 0,
        jnp.concatenate([row_block, other_block], axis=2),
        jnp.concatenate([other_block, row_block], axis=2),
    )
    products = jnp.einsum(
        "kqib,krjb->kqrij", row_block, col_block, preferred_element_type=jnp.float32
    )
    real_part = (products[:, 0, 0] + products[:, 1, 1]) / blocks
    imag_part = (products[:, 1, 0] - products[:, 0, 1]) / blocks
    return jnp.stack([real_part, imag_part], axis=1).astype(jnp.bfloat16)[None]


GROUP = 8
LANES = 128


def wide_table(fft_length, channels):
    n = np.arange(fft_length, dtype=np.int64)[:, None]
    k = np.arange(channels, dtype=np.int64)[None, :]
    phase = (n * k % fft_length).astype(np.float32) * np.float32(2.0 * math.pi / fft_length)
    scale = np.float32(1.0 / math.sqrt(fft_length))
    cosine = (np.cos(phase) * scale).astype(jnp.bfloat16)
    sine = (np.sin(phase) * scale).astype(jnp.bfloat16)
    upper = np.concatenate([cosine, -sine], axis=1)
    lower = np.concatenate([sine, cosine], axis=1)
    whole = np.concatenate([upper, lower], axis=0)
    return np.concatenate([whole] * (LANES // (2 * channels)), axis=1)


def row_cuts(groups):
    return [0] + list(range(1, groups, 2)) + [groups]


def iota(shape, dim):
    return lax.broadcasted_iota(jnp.int32, shape, dim)


def slot_columns(owner_ref, channels, capacity):
    square = iota((channels, channels), 0) == iota((channels, channels), 1)
    col = jnp.sum(jnp.where(square, owner_ref[...], 0), axis=1, keepdims=True)
    lane = iota((channels, LANES), 1)
    channel = lane % channels
    row_number = iota((channels, LANES), 0)
    owner = jnp.sum(jnp.where(row_number == channel, col, 0), axis=0, keepdims=True)
    rank = jnp.sum(
        jnp.where((col == owner) & (row_number < channel), 1, 0), axis=0, keepdims=True
    )
    lane = iota((1, LANES), 1)
    place = (owner * capacity + rank) * 2 + lane // channels
    place = jnp.where(lane < 2 * channels, place, -1)
    hot = jnp.where(iota((LANES, LANES), 0) == place, 1.0, 0.0)
    return hot.T.astype(jnp.bfloat16)


def block_transpose(parts, width):
    count = len(parts)
    lane = iota(parts[0].shape, 1) // width
    half = 1
    while half < count:
        low = lane // half % 2 == 0
        out = list(parts)
        for i in range(count):
            if i // half % 2 == 0:
                a, b = parts[i], parts[i + half]
                out[i] = jnp.where(low, a, pltpu.roll(b, half * width, 1))
                out[i + half] = jnp.where(low, pltpu.roll(a, LANES - half * width, 1), b)
        parts = out
        half *= 2
    return parts


def channelize_kernel(
    sizes, v_ref, taps_hbm, table_hbm, owner_hbm, marks_hbm, x_ref,
    taps_ref, table_ref, owner_ref, marks_ref, small_sem, vbuf, wbuf, zbuf, sendbuf, in_sem, send_sem, recv_sem, own_sem, pass_send, pass_recv,
):
    stations, span, samples, taps, blocks, channels, owners, capacity, tm_count = sizes
    cuts = row_cuts(blocks // GROUP)
    steps = len(cuts) - 1
    width = 2 * capacity
    pol = lax.axis_index("pol")
    me = lax.axis_index("stn") * tm_count + lax.axis_index("tm")
    ends = [0] + [cut * GROUP + taps - 1 for cut in cuts[1:]]

    small = [
        pltpu.make_async_copy(source, target, small_sem.at[i])
        for i, (source, target) in enumerate((
            (taps_hbm, taps_ref), (table_hbm, table_ref), (owner_hbm, owner_ref),
            (marks_hbm, marks_ref),
        ))
    ]
    for load in small:
        load.start()
    loads = []
    for c in range(steps):
        rows = pl.ds(ends[c], ends[c + 1] - ends[c])
        load = pltpu.make_async_copy(v_ref.at[rows], vbuf.at[rows], in_sem.at[c])
        loads.append(load)
    loads[0].start()

    barrier = pltpu.get_barrier_semaphore()
    for k in range(1, owners):
        peer = lax.rem(me + k, owners)
        pl.semaphore_signal(
            barrier, inc=1, device_id={"stn": peer // tm_count, "tm": lax.rem(peer, tm_count)},
            device_id_type=pl.DeviceIdType.MESH,
        )
    pl.semaphore_signal(
        barrier, inc=1, device_id={"pol": 1 - pol}, device_id_type=pl.DeviceIdType.MESH
    )

    for load in small:
        load.wait()
    loads[1].start()
    columns = taps * 2 * channels
    expand = jnp.where(
        iota((taps, columns), 0) == iota((taps, columns), 1) // (2 * channels), 1.0, 0.0
    ).astype(jnp.bfloat16)
    half = samples // 2
    piece = 256
    for i in range(half // piece):
        tap_rows = lax.dot_general(
            taps_ref[:, i * piece : (i + 1) * piece], expand,
            (((0,), (0,)), ((), ())), preferred_element_type=jnp.float32,
        )
        for base in (0, half):
            at = slice(base + i * piece, base + (i + 1) * piece)
            entry = table_ref[at, :].astype(jnp.float32)
            for j in range(columns // LANES):
                lanes = slice(j * LANES, (j + 1) * LANES)
                wbuf[at, lanes] = (tap_rows[:, lanes] * entry).astype(jnp.bfloat16)

    for load in loads[2:]:
        load.start()
    pick = slot_columns(owner_ref, channels, capacity)
    diagonal = iota((stations, stations), 0) == iota((stations, stations), 1)
    keep = 1.0 - jnp.sum(
        jnp.where(diagonal, marks_ref[...], 0), axis=1, keepdims=True
    ).astype(jnp.float32)
    pl.semaphore_wait(barrier, owners)

    def shifted(b):
        total = None
        for j in range(columns // LANES):
            row = b + 2 * j
            term = zbuf[row * stations : (row + 1) * stations, j * LANES : (j + 1) * LANES]
            total = term if total is None else total + term
        return total

    sends, passes = [], []

    def send_groups(c, first, last):
        batch_groups = pl.ds(first, last - first)
        for g in range(first, last):
            summed = [shifted(g * GROUP + i) for i in range(GROUP + 1)]
            spectra = [
                ((summed[i] + pltpu.roll(summed[i + 1], 2 * channels, 1)) * keep).astype(jnp.bfloat16)
                for i in range(GROUP)
            ]
            placed = jnp.dot(
                jnp.concatenate(spectra, axis=0), pick, preferred_element_type=jnp.float32
            )
            parts = [placed[i * stations : (i + 1) * stations] for i in range(GROUP)]
            for o, part in enumerate(block_transpose(parts, width)):
                sendbuf[o, g] = part.astype(jnp.bfloat16)
        batch = []
        for k in range(1, owners):
            peer = lax.rem(me + k, owners)
            copy = pltpu.make_async_remote_copy(
                src_ref=sendbuf.at[peer, batch_groups],
                dst_ref=x_ref.at[pol, me, batch_groups],
                send_sem=send_sem.at[c, k],
                recv_sem=recv_sem.at[c, k],
                device_id={"stn": peer // tm_count, "tm": lax.rem(peer, tm_count)},
                device_id_type=pl.DeviceIdType.MESH,
            )
            copy.start()
            batch.append(copy)
        own = pltpu.make_async_copy(
            sendbuf.at[me, batch_groups], x_ref.at[pol, me, batch_groups], own_sem.at[c]
        )
        own.start()
        sends.append((batch, own, batch_groups))

    def pass_on(c):
        batch, own, batch_groups = sends[c]
        own.wait()
        for k in range(1, owners):
            source = lax.rem(me + owners - k, owners)
            here = x_ref.at[pol, source, batch_groups]
            pltpu.make_async_copy(here, here, recv_sem.at[c, k]).wait()
        mine = x_ref.at[pol, :, batch_groups]
        copy = pltpu.make_async_remote_copy(
            src_ref=mine, dst_ref=mine, send_sem=pass_send.at[c], recv_sem=pass_recv.at[c],
            device_id={"pol": 1 - pol}, device_id_type=pl.DeviceIdType.MESH,
        )
        copy.start()
        passes.append(copy)

    for c in range(steps):
        loads[c].wait()
        first, last = ends[c], ends[c + 1]
        zbuf[first * stations : last * stations, :] = jnp.dot(
            vbuf[first:last].reshape((last - first) * stations, samples), wbuf[...],
            preferred_element_type=jnp.float32,
        )
        send_groups(c, cuts[c], cuts[c + 1])
    for c in range(steps):
        pass_on(c)
    for batch, own, batch_groups in sends:
        for copy in batch:
            copy.wait_send()
    for copy in passes:
        copy.wait()


def correlate_kernel(blocks, capacity, x_ref, out_ref, held, result, out_sem):
    pol = lax.axis_index("pol")
    _, owners, groups, stations, _ = x_ref.shape
    rows = owners * stations
    lane = iota((1, LANES), 1)
    straight, turned = [], []
    for g in range(groups):
        every = x_ref[:, :, g].reshape(2 * rows, LANES).astype(jnp.float32)
        held[g * LANES : (g + 1) * LANES, :] = every.T.astype(jnp.bfloat16)
        left = x_ref[pol, :, g].reshape(rows, LANES)
        wide = left.astype(jnp.float32)
        swapped = jnp.where(
            lane % 2 == 0, pltpu.roll(wide, LANES - 1, 1), -pltpu.roll(wide, 1, 1)
        )
        straight.append(left)
        turned.append(swapped.astype(jnp.bfloat16))
    operands = [jnp.concatenate(tiles, axis=1) for tiles in (straight, turned)]
    lane = iota((1, groups * LANES), 1)
    copies = []
    for k in range(capacity):
        mask = jnp.where(lane % (2 * capacity) // 2 == k, 1.0, 0.0).astype(jnp.bfloat16)
        for q, operand in enumerate(operands):
            product = jnp.dot(operand * mask, held[...], preferred_element_type=jnp.float32)
            result[k, q] = (product * (1.0 / blocks)).astype(jnp.bfloat16)
        copy = pltpu.make_async_copy(result.at[k], out_ref.at[0, k], out_sem.at[k])
        copy.start()
        copies.append(copy)
    for copy in copies:
        copy.wait()


def fast_body(voltages, fir_taps, owner_map, station_flag_marks):
    stations, _, span, samples = voltages.shape
    taps = fir_taps.shape[0]
    blocks = span - taps + 1
    channels = owner_map.shape[0]
    tm_count = lax.axis_size("tm")
    owners = lax.axis_size("stn") * tm_count
    capacity = 2 * channels // owners
    groups = blocks // GROUP
    steps = len(row_cuts(groups)) - 1
    columns = taps * 2 * channels
    sizes = (stations, span, samples, taps, blocks, channels, owners, capacity, tm_count)
    vmem = pl.BlockSpec(memory_space=pltpu.VMEM)
    dma = pltpu.SemaphoreType.DMA
    x = pl.pallas_call(
        functools.partial(channelize_kernel, sizes),
        out_shape=jax.ShapeDtypeStruct((2, owners, groups, stations, LANES), jnp.bfloat16),
        in_specs=[pl.BlockSpec(memory_space=pltpu.HBM)] * 5,
        out_specs=vmem,
        scratch_shapes=[
            pltpu.VMEM(fir_taps.shape, jnp.bfloat16),
            pltpu.VMEM((samples, LANES), jnp.bfloat16),
            pltpu.VMEM((1, channels), jnp.int32),
            pltpu.VMEM((1, stations), jnp.int32),
            dma((4,)),
            pltpu.VMEM((span, stations, samples), jnp.bfloat16),
            pltpu.VMEM((samples, columns), jnp.bfloat16),
            pltpu.VMEM((span * stations, columns), jnp.float32),
            pltpu.VMEM((owners, groups, stations, LANES), jnp.bfloat16),
            dma((steps,)),
            dma((steps, owners)),
            dma((steps, owners)),
            dma((steps,)),
            dma((steps,)),
            dma((steps,)),
        ],
        compiler_params=pltpu.CompilerParams(
            collective_id=0, has_side_effects=True, vmem_limit_bytes=60 * 1024 * 1024
        ),
        name="channelize",
    )(
        jnp.transpose(voltages[:, 0], (1, 0, 2)), fir_taps, jnp.asarray(wide_table(samples // 2, channels)),
        owner_map.reshape(1, channels),
        station_flag_marks.reshape(1, stations),
    )
    rows = owners * stations
    return pl.pallas_call(
        functools.partial(correlate_kernel, blocks, capacity),
        out_shape=jax.ShapeDtypeStruct((1, capacity, 2, rows, 2 * rows), jnp.bfloat16),
        in_specs=[vmem],
        out_specs=pl.BlockSpec(memory_space=pl.ANY),
        scratch_shapes=[
            pltpu.VMEM((groups * LANES, 2 * rows), jnp.bfloat16),
            pltpu.VMEM((capacity, 2, rows, 2 * rows), jnp.bfloat16),
            dma((capacity,)),
        ],
        compiler_params=pltpu.CompilerParams(vmem_limit_bytes=24 * 1024 * 1024),
        name="correlate",
    )(x)


def body(voltages, fir_taps, owner_map, station_flag_marks):
    stations, _, span, samples = voltages.shape
    taps = fir_taps.shape[0]
    channels = owner_map.shape[0]
    blocks = span - taps + 1
    owners = lax.axis_size("stn") * lax.axis_size("tm")
    width = 4 * channels // owners
    fits = (
        4 * channels == LANES
        and owners * width == LANES
        and GROUP * width == LANES
        and taps == GROUP
        and blocks % GROUP == 0
        and blocks <= LANES // 2
        and width % 4 == 0
        and blocks >= 2 * GROUP
        and stations % 16 == 0
        and samples % 512 == 0
        and lax.axis_size("pol") == 2
    )
    run = fast_body if fits else general_body
    return run(voltages, fir_taps, owner_map, station_flag_marks)


def solution(mesh):
    in_specs = (P(("group", "stn", "tm"), "pol", None, None), P(), P(), P(("stn", "tm")))
    out_specs = P(("group", "stn", "tm"), None, None, "pol", None)
    return jax.shard_map(body, mesh=mesh, in_specs=in_specs, out_specs=out_specs, check_vma=False)
```

```python
import functools
import math

import jax
import jax.numpy as jnp
import numpy as np
from jax import lax
from jax.experimental import pallas as pl
from jax.experimental.pallas import tpu as pltpu
from jax.sharding import PartitionSpec as P


def partner(value, axis, stride):
    return lax.ppermute(value, axis, [(i, i ^ 1 << stride) for i in range(lax.axis_size(axis))])


def dft_table(fft_length, channels):
    row_numbers = jnp.arange(fft_length, dtype=jnp.int32)[:, None]
    col_ids = jnp.arange(channels, dtype=jnp.int32)[None, :]
    phase_idx = (row_numbers * col_ids % fft_length).astype(jnp.float32) * (
        2.0 * math.pi / fft_length
    )
    norm_scale = 1.0 / math.sqrt(fft_length)
    cosine = (jnp.cos(phase_idx) * norm_scale).astype(jnp.bfloat16)
    sine_part = (jnp.sin(phase_idx) * norm_scale).astype(jnp.bfloat16)
    upper_rows = jnp.concatenate([cosine, -sine_part], axis=1)
    lower_rows = jnp.concatenate([sine_part, cosine], axis=1)
    return jnp.concatenate([upper_rows, lower_rows], axis=0)


def slot_matches(route_map, owners, capacity):
    channels = route_map.shape[0]
    position = jnp.arange(channels, dtype=jnp.int32)
    earlier = (route_map[:, None] == route_map[None, :]) & (position[None, :] < position[:, None])
    position_within_owner = jnp.sum(earlier.astype(jnp.int32), axis=1)
    owner_ids = jnp.arange(owners, dtype=jnp.int32)
    slot_ids = jnp.arange(capacity, dtype=jnp.int32)
    return (route_map[None, None, :] == owner_ids[:, None, None]) & (
        position_within_owner[None, None, :] == slot_ids[None, :, None]
    )


def corner_turn(outgoing):
    return lax.all_to_all(outgoing, ("stn", "tm"), split_axis=3, concat_axis=3, tiled=True)


def general_body(voltages, fir_taps, owner_map, station_flag_marks):
    st_dev = voltages.shape[0]
    span_blocks = voltages.shape[2]
    fft_length = voltages.shape[3] // 2
    tap_count = fir_taps.shape[0]
    blocks = span_blocks - tap_count + 1
    channels = owner_map.shape[0]
    stn_count = lax.axis_size("stn")
    tm_count = lax.axis_size("tm")
    owners = stn_count * tm_count
    capacity = 2 * channels // owners
    stations = st_dev * owners
    pol_index = lax.axis_index("pol")
    table = dft_table(fft_length, channels)
    wide_taps = jnp.concatenate([fir_taps, fir_taps], axis=1).astype(jnp.float32)
    samples = voltages[:, 0]
    filtered = wide_taps[0] * samples[:, 0:blocks].astype(jnp.float32)
    for tap_index in range(1, tap_count):
        filtered = filtered + wide_taps[tap_index] * samples[
            :, tap_index : tap_index + blocks
        ].astype(jnp.float32)
    flat_rows = filtered.astype(jnp.bfloat16).reshape(st_dev * blocks, 2 * fft_length)
    single_spectrum = jnp.dot(flat_rows, table, preferred_element_type=jnp.float32).reshape(
        st_dev, blocks, 2, channels
    )
    clean_stations = (1 - station_flag_marks).astype(jnp.float32)
    channel_spectra = (single_spectrum * clean_stations[:, None, None, None]).astype(jnp.bfloat16)
    pick_matrix = slot_matches(owner_map[:, 0], owners, capacity).astype(jnp.bfloat16)
    outgoing = jnp.einsum(
        "okc,sbqc->kqosb", pick_matrix, channel_spectra, preferred_element_type=jnp.float32
    )
    outgoing = outgoing.astype(jnp.bfloat16).reshape(capacity, 2, 1, owners, st_dev * blocks)
    arrived = corner_turn(outgoing)
    row_block = arrived.reshape(capacity, 2, stations, blocks)
    other_block = partner(row_block, "pol", 0)
    col_block = jnp.where(
        pol_index == 0,
        jnp.concatenate([row_block, other_block], axis=2),
        jnp.concatenate([other_block, row_block], axis=2),
    )
    products = jnp.einsum(
        "kqib,krjb->kqrij", row_block, col_block, preferred_element_type=jnp.float32
    )
    real_part = (products[:, 0, 0] + products[:, 1, 1]) / blocks
    imag_part = (products[:, 1, 0] - products[:, 0, 1]) / blocks
    return jnp.stack([real_part, imag_part], axis=1).astype(jnp.bfloat16)[None]


GROUP = 8
LANES = 128


def wide_table(fft_length, channels):
    n = np.arange(fft_length, dtype=np.int64)[:, None]
    k = np.arange(channels, dtype=np.int64)[None, :]
    phase = (n * k % fft_length).astype(np.float32) * np.float32(2.0 * math.pi / fft_length)
    scale = np.float32(1.0 / math.sqrt(fft_length))
    cosine = (np.cos(phase) * scale).astype(jnp.bfloat16)
    sine = (np.sin(phase) * scale).astype(jnp.bfloat16)
    upper = np.concatenate([cosine, -sine], axis=1)
    lower = np.concatenate([sine, cosine], axis=1)
    whole = np.concatenate([upper, lower], axis=0)
    return np.concatenate([whole] * (LANES // (2 * channels)), axis=1)


def row_cuts(groups):
    return [0] + list(range(1, groups, 2)) + [groups]


def iota(shape, dim):
    return lax.broadcasted_iota(jnp.int32, shape, dim)


def slot_columns(owner_ref, channels, capacity):
    square = iota((channels, channels), 0) == iota((channels, channels), 1)
    col = jnp.sum(jnp.where(square, owner_ref[...], 0), axis=1, keepdims=True)
    lane = iota((channels, LANES), 1)
    channel = lane % channels
    row_number = iota((channels, LANES), 0)
    owner = jnp.sum(jnp.where(row_number == channel, col, 0), axis=0, keepdims=True)
    rank = jnp.sum(
        jnp.where((col == owner) & (row_number < channel), 1, 0), axis=0, keepdims=True
    )
    lane = iota((1, LANES), 1)
    place = (owner * capacity + rank) * 2 + lane // channels
    place = jnp.where(lane < 2 * channels, place, -1)
    hot = jnp.where(iota((LANES, LANES), 0) == place, 1.0, 0.0)
    return hot.T.astype(jnp.bfloat16)


def block_transpose(parts, width):
    count = len(parts)
    lane = iota(parts[0].shape, 1) // width
    half = 1
    while half < count:
        low = lane // half % 2 == 0
        out = list(parts)
        for i in range(count):
            if i // half % 2 == 0:
                a, b = parts[i], parts[i + half]
                out[i] = jnp.where(low, a, pltpu.roll(b, half * width, 1))
                out[i + half] = jnp.where(low, pltpu.roll(a, LANES - half * width, 1), b)
        parts = out
        half *= 2
    return parts


def channelize_kernel(
    sizes, v_ref, taps_hbm, table_hbm, owner_hbm, marks_hbm, x_ref,
    taps_ref, table_ref, owner_ref, marks_ref, small_sem, vbuf, wbuf, zbuf, sendbuf, in_sem, send_sem, recv_sem, own_sem, pass_send, pass_recv,
):
    stations, span, samples, taps, blocks, channels, owners, capacity, tm_count = sizes
    cuts = row_cuts(blocks // GROUP)
    steps = len(cuts) - 1
    width = 2 * capacity
    pol = lax.axis_index("pol")
    me = lax.axis_index("stn") * tm_count + lax.axis_index("tm")
    ends = [0] + [cut * GROUP + taps - 1 for cut in cuts[1:]]

    small = [
        pltpu.make_async_copy(source, target, small_sem.at[i])
        for i, (source, target) in enumerate((
            (taps_hbm, taps_ref), (table_hbm, table_ref), (owner_hbm, owner_ref),
            (marks_hbm, marks_ref),
        ))
    ]
    for load in small:
        load.start()
    loads = []
    for c in range(steps):
        rows = pl.ds(ends[c], ends[c + 1] - ends[c])
        load = pltpu.make_async_copy(v_ref.at[rows], vbuf.at[rows], in_sem.at[c])
        loads.append(load)
    loads[0].start()

    barrier = pltpu.get_barrier_semaphore()
    for k in range(1, owners):
        peer = lax.rem(me + k, owners)
        pl.semaphore_signal(
            barrier, inc=1, device_id={"stn": peer // tm_count, "tm": lax.rem(peer, tm_count)},
            device_id_type=pl.DeviceIdType.MESH,
        )
    pl.semaphore_signal(
        barrier, inc=1, device_id={"pol": 1 - pol}, device_id_type=pl.DeviceIdType.MESH
    )

    for load in small:
        load.wait()
    loads[1].start()
    columns = taps * 2 * channels
    expand = jnp.where(
        iota((taps, columns), 0) == iota((taps, columns), 1) // (2 * channels), 1.0, 0.0
    ).astype(jnp.bfloat16)
    half = samples // 2
    piece = 256
    for i in range(half // piece):
        tap_rows = lax.dot_general(
            taps_ref[:, i * piece : (i + 1) * piece], expand,
            (((0,), (0,)), ((), ())), preferred_element_type=jnp.float32,
        )
        for base in (0, half):
            at = slice(base + i * piece, base + (i + 1) * piece)
            entry = table_ref[at, :].astype(jnp.float32)
            for j in range(columns // LANES):
                lanes = slice(j * LANES, (j + 1) * LANES)
                wbuf[at, lanes] = (tap_rows[:, lanes] * entry).astype(jnp.bfloat16)

    for load in loads[2:]:
        load.start()
    pick = slot_columns(owner_ref, channels, capacity)
    diagonal = iota((stations, stations), 0) == iota((stations, stations), 1)
    keep = 1.0 - jnp.sum(
        jnp.where(diagonal, marks_ref[...], 0), axis=1, keepdims=True
    ).astype(jnp.float32)
    pl.semaphore_wait(barrier, owners)

    def shifted(b):
        total = None
        for j in range(columns // LANES):
            row = b + 2 * j
            term = zbuf[row * stations : (row + 1) * stations, j * LANES : (j + 1) * LANES]
            total = term if total is None else total + term
        return total

    sends, passes = [], []

    def send_groups(c, first, last):
        batch_groups = pl.ds(first, last - first)
        for g in range(first, last):
            summed = [shifted(g * GROUP + i) for i in range(GROUP + 1)]
            spectra = [
                ((summed[i] + pltpu.roll(summed[i + 1], 2 * channels, 1)) * keep).astype(jnp.bfloat16)
                for i in range(GROUP)
            ]
            placed = jnp.dot(
                jnp.concatenate(spectra, axis=0), pick, preferred_element_type=jnp.float32
            )
            parts = [placed[i * stations : (i + 1) * stations] for i in range(GROUP)]
            for o, part in enumerate(block_transpose(parts, width)):
                sendbuf[o, g] = part.astype(jnp.bfloat16)
        batch = []
        for k in range(1, owners):
            peer = lax.rem(me + k, owners)
            copy = pltpu.make_async_remote_copy(
                src_ref=sendbuf.at[peer, batch_groups],
                dst_ref=x_ref.at[pol, me, batch_groups],
                send_sem=send_sem.at[c, k],
                recv_sem=recv_sem.at[c, k],
                device_id={"stn": peer // tm_count, "tm": lax.rem(peer, tm_count)},
                device_id_type=pl.DeviceIdType.MESH,
            )
            copy.start()
            batch.append(copy)
        own = pltpu.make_async_copy(
            sendbuf.at[me, batch_groups], x_ref.at[pol, me, batch_groups], own_sem.at[c]
        )
        own.start()
        sends.append((batch, own, batch_groups))

    def pass_on(c):
        batch, own, batch_groups = sends[c]
        own.wait()
        for k in range(1, owners):
            source = lax.rem(me + owners - k, owners)
            here = x_ref.at[pol, source, batch_groups]
            pltpu.make_async_copy(here, here, recv_sem.at[c, k]).wait()
        mine = x_ref.at[pol, :, batch_groups]
        copy = pltpu.make_async_remote_copy(
            src_ref=mine, dst_ref=mine, send_sem=pass_send.at[c], recv_sem=pass_recv.at[c],
            device_id={"pol": 1 - pol}, device_id_type=pl.DeviceIdType.MESH,
        )
        copy.start()
        passes.append(copy)

    for c in range(steps):
        loads[c].wait()
        first, last = ends[c], ends[c + 1]
        zbuf[first * stations : last * stations, :] = jnp.dot(
            vbuf[first:last].reshape((last - first) * stations, samples), wbuf[...],
            preferred_element_type=jnp.float32,
        )
        send_groups(c, cuts[c], cuts[c + 1])
        if c >= 2:
            pass_on(c - 2)
    for c in range(max(steps - 2, 0), steps):
        pass_on(c)
    for batch, own, batch_groups in sends:
        for copy in batch:
            copy.wait_send()
    for copy in passes:
        copy.wait()


def correlate_kernel(blocks, capacity, x_ref, out_ref, held, result, out_sem):
    pol = lax.axis_index("pol")
    _, owners, groups, stations, _ = x_ref.shape
    rows = owners * stations
    lane = iota((1, LANES), 1)
    straight, turned = [], []
    for g in range(groups):
        every = x_ref[:, :, g].reshape(2 * rows, LANES).astype(jnp.float32)
        held[g * LANES : (g + 1) * LANES, :] = every.T.astype(jnp.bfloat16)
        left = x_ref[pol, :, g].reshape(rows, LANES)
        wide = left.astype(jnp.float32)
        swapped = jnp.where(
            lane % 2 == 0, pltpu.roll(wide, LANES - 1, 1), -pltpu.roll(wide, 1, 1)
        )
        straight.append(left)
        turned.append(swapped.astype(jnp.bfloat16))
    operands = [jnp.concatenate(tiles, axis=1) for tiles in (straight, turned)]
    lane = iota((1, groups * LANES), 1)
    copies = []
    for k in range(capacity):
        mask = jnp.where(lane % (2 * capacity) // 2 == k, 1.0, 0.0).astype(jnp.bfloat16)
        for q, operand in enumerate(operands):
            product = jnp.dot(operand * mask, held[...], preferred_element_type=jnp.float32)
            result[k, q] = (product * (1.0 / blocks)).astype(jnp.bfloat16)
        copy = pltpu.make_async_copy(result.at[k], out_ref.at[0, k], out_sem.at[k])
        copy.start()
        copies.append(copy)
    for copy in copies:
        copy.wait()


def fast_body(voltages, fir_taps, owner_map, station_flag_marks):
    stations, _, span, samples = voltages.shape
    taps = fir_taps.shape[0]
    blocks = span - taps + 1
    channels = owner_map.shape[0]
    tm_count = lax.axis_size("tm")
    owners = lax.axis_size("stn") * tm_count
    capacity = 2 * channels // owners
    groups = blocks // GROUP
    steps = len(row_cuts(groups)) - 1
    columns = taps * 2 * channels
    sizes = (stations, span, samples, taps, blocks, channels, owners, capacity, tm_count)
    vmem = pl.BlockSpec(memory_space=pltpu.VMEM)
    dma = pltpu.SemaphoreType.DMA
    x = pl.pallas_call(
        functools.partial(channelize_kernel, sizes),
        out_shape=jax.ShapeDtypeStruct((2, owners, groups, stations, LANES), jnp.bfloat16),
        in_specs=[pl.BlockSpec(memory_space=pltpu.HBM)] * 5,
        out_specs=vmem,
        scratch_shapes=[
            pltpu.VMEM(fir_taps.shape, jnp.bfloat16),
            pltpu.VMEM((samples, LANES), jnp.bfloat16),
            pltpu.VMEM((1, channels), jnp.int32),
            pltpu.VMEM((1, stations), jnp.int32),
            dma((4,)),
            pltpu.VMEM((span, stations, samples), jnp.bfloat16),
            pltpu.VMEM((samples, columns), jnp.bfloat16),
            pltpu.VMEM((span * stations, columns), jnp.float32),
            pltpu.VMEM((owners, groups, stations, LANES), jnp.bfloat16),
            dma((steps,)),
            dma((steps, owners)),
            dma((steps, owners)),
            dma((steps,)),
            dma((steps,)),
            dma((steps,)),
        ],
        compiler_params=pltpu.CompilerParams(
            collective_id=0, has_side_effects=True, vmem_limit_bytes=60 * 1024 * 1024
        ),
        name="channelize",
    )(
        jnp.transpose(voltages[:, 0], (1, 0, 2)), fir_taps, jnp.asarray(wide_table(samples // 2, channels)),
        owner_map.reshape(1, channels),
        station_flag_marks.reshape(1, stations),
    )
    rows = owners * stations
    return pl.pallas_call(
        functools.partial(correlate_kernel, blocks, capacity),
        out_shape=jax.ShapeDtypeStruct((1, capacity, 2, rows, 2 * rows), jnp.bfloat16),
        in_specs=[vmem],
        out_specs=pl.BlockSpec(memory_space=pl.ANY),
        scratch_shapes=[
            pltpu.VMEM((groups * LANES, 2 * rows), jnp.bfloat16),
            pltpu.VMEM((capacity, 2, rows, 2 * rows), jnp.bfloat16),
            dma((capacity,)),
        ],
        compiler_params=pltpu.CompilerParams(vmem_limit_bytes=24 * 1024 * 1024),
        name="correlate",
    )(x)


def body(voltages, fir_taps, owner_map, station_flag_marks):
    stations, _, span, samples = voltages.shape
    taps = fir_taps.shape[0]
    channels = owner_map.shape[0]
    blocks = span - taps + 1
    owners = lax.axis_size("stn") * lax.axis_size("tm")
    width = 4 * channels // owners
    fits = (
        4 * channels == LANES
        and owners * width == LANES
        and GROUP * width == LANES
        and taps == GROUP
        and blocks % GROUP == 0
        and blocks <= LANES // 2
        and width % 4 == 0
        and blocks >= 2 * GROUP
        and stations % 16 == 0
        and samples % 512 == 0
        and lax.axis_size("pol") == 2
    )
    run = fast_body if fits else general_body
    return run(voltages, fir_taps, owner_map, station_flag_marks)


def solution(mesh):
    in_specs = (P(("group", "stn", "tm"), "pol", None, None), P(), P(), P(("stn", "tm")))
    out_specs = P(("group", "stn", "tm"), None, None, "pol", None)
    return jax.shard_map(body, mesh=mesh, in_specs=in_specs, out_specs=out_specs, check_vma=False)
```
